256 devices in a mesh: cache: 64 (over x, z, core), tensor: 4 (over y).
Axes of the slice: x: 4, y: 4, z: 8, core: 2. Of those that a mesh axis runs over, the one named last changes fastest.
Arguments:
- queries: bfloat16 [64, 256, 2048], P('cache', None, 'tensor'), may hold values from -36 to 36
- own_keys: bfloat16 [64, 256, 512], P('cache', None, 'tensor'), may hold values from -12 to 12
- own_values: bfloat16 [64, 256, 512], P('cache', None, 'tensor'), may hold values from -6 to 6
- passage_keys: bfloat16 [1024, 512, 512], P('cache', None, 'tensor'), may hold values from -12 to 12
- passage_values: bfloat16 [1024, 512, 512], P('cache', None, 'tensor'), may hold values from -6 to 6
- passage_slot: int32 [1024], replicated, may hold values from 0 to 1023, as said below
- picks: int32 [64, 16], P('cache'), may hold values from 0 to 1023, as said below
- lengths: int32 [64], P('cache'), may hold values from 64 to 256, as said below
- residual: bfloat16 [64, 256, 4096], P('cache', None, 'tensor'), may hold values from -0.59765625 to 0.59765625
- out_weight: bfloat16 [2048, 4096], P('tensor'), may hold values from -0.5 to 0.5
Outputs:
- mixed_out: bfloat16 [64, 256, 4096], P('cache', None, 'tensor')
The draws below stay inside these ranges and needn't reach their ends.
Inputs may be any that keep to these rules, and one draw needn't show every extreme that they name: A permutation: passage id p is stored at row passage_slot[p]; storage row s lies on index s // 16 of cache. `picks`: the 16 ids of one request are different; at most 1 of them have storage rows on one index of cache, and some request has exactly 1 on some index. `lengths`: some request has 256 real rows.
All inputs are finite; a program needn't handle non-finite values.
Results may differ from the reference program's by a relative error of at most 0.0052.
Values may be sent and summed in bfloat16 or wider, within the bound.
No kernel may reach another device: no remote copies, remote signals or barrier semaphores. Data moves between devices by JAX's collectives and lax.ppermute only.
A program may use at most 192 MiB of HBM per device.

```python
import math
import jax
import jax.numpy as jnp
from jax import lax

D = 4096
HD = 128
QH = 16
KVH = 4
PLEN = 512
PICKS = 16
QLEN = 256
PASS_DEV = 16
REQS = 64
PASSAGES = 1024
CAPP = 1


def storage_table(key):
    return jax.random.permutation(key, PASSAGES).astype(jnp.int32)


def draw_passage_slot(key, part):
    table = storage_table(key)
    return table


def draw_picks(key, part):
    table = storage_table(key)
    key = jax.random.fold_in(key, 7)
    first, second, third = jax.random.split(key, 3)
    owners_all = PASSAGES // PASS_DEV
    columns = owners_all * CAPP
    ranking = jax.random.permutation(first, owners_all).astype(jnp.int32)
    favour = (owners_all - 1 - ranking) * 8192 // owners_all
    column_ids = jnp.arange(columns, dtype=jnp.int32)
    noise = jax.random.randint(second, (REQS, columns), 0, 4096, dtype=jnp.int32)
    scores = (noise + favour[column_ids // CAPP][None, :]) * columns + column_ids[None, :]
    unused, chosen = jax.lax.top_k(scores, PICKS)
    owner_ids = chosen // CAPP
    copy_ids = chosen % CAPP
    offsets = jax.random.randint(third, (REQS, owners_all), 0, PASS_DEV, dtype=jnp.int32)
    base_local = jnp.take_along_axis(offsets, owner_ids, axis=1)
    local_ids = (base_local + copy_ids) % PASS_DEV
    storage_rows = owner_ids * PASS_DEV + local_ids
    inverse = jnp.zeros((PASSAGES,), jnp.int32).at[table].set(jnp.arange(PASSAGES, dtype=jnp.int32))
    return inverse[storage_rows].astype(jnp.int32)


def draw_lengths(key, part):
    key = jax.random.fold_in(key, 9)
    first, second = jax.random.split(key)
    spans = jax.random.randint(first, (REQS,), QLEN // 4, QLEN + 1, dtype=jnp.int32)
    longest = jax.random.randint(second, (), 0, REQS, dtype=jnp.int32)
    return spans.at[longest].set(QLEN)


def draw_own_keys(key, part):
    key = jax.random.fold_in(key, 3)
    values = jax.random.normal(key, (REQS, QLEN, KVH * HD), jnp.float32)
    return jnp.clip(values, -12.0, 12.0).astype(jnp.bfloat16)


def draw_passage_keys(key, part):
    key = jax.random.fold_in(key, 5)
    values = jax.random.normal(key, (PASSAGES, PLEN, KVH * HD), jnp.float32)
    return jnp.clip(values, -12.0, 12.0).astype(jnp.bfloat16)


def draw_queries(key, part):
    key = jax.random.fold_in(key, 4)
    values = jax.random.normal(key, (REQS, QLEN, QH * HD), jnp.float32)
    return jnp.clip(values, -36.0, 36.0).astype(jnp.bfloat16)


def steps_of(key, dims, pieces, smallest, top_value):
    factor_of, own = 1.0, jax.random.fold_in(key, 6)
    for dim, blocks in pieces:
        draws = jnp.exp(jax.random.uniform(jax.random.fold_in(own, dim), (blocks,), jnp.float32, smallest / len(pieces), top_value / len(pieces)))
        factor_of = factor_of * jnp.repeat(draws, dims[dim] // blocks).reshape([-1 if axis == dim else 1 for axis in range(len(dims))])
    return factor_of


def normal_values(key, extent, deviation, reach, shards=(), kind=jnp.bfloat16):
    drawn = deviation * jax.random.normal(key, extent, jnp.float32)
    if shards:
        drawn = drawn * steps_of(key, extent, shards, -0.22, 0.18)
    return jnp.clip(drawn, -reach, reach).astype(kind)


def setup_inputs(seed: int = 0) -> dict:
    key_of = jax.random.split(jax.random.key(seed), 11)
    return {
        "queries": draw_queries(jax.random.fold_in(key_of[10], 71), 0),
        "own_keys": draw_own_keys(jax.random.fold_in(key_of[10], 71), 0),
        "own_values": normal_values(key_of[2], (REQS, QLEN, KVH * HD), 1.0, 6.0, ((0, 64), (2, 4))),
        "passage_keys": draw_passage_keys(jax.random.fold_in(key_of[10], 71), 0),
        "passage_values": normal_values(key_of[4], (PASSAGES, PLEN, KVH * HD), 1.0, 6.0, ((0, 64), (2, 4))),
        "passage_slot": draw_passage_slot(jax.random.fold_in(key_of[10], 71), 0),
        "picks": draw_picks(jax.random.fold_in(key_of[10], 71), 0),
        "lengths": draw_lengths(jax.random.fold_in(key_of[10], 71), 0),
        "residual": normal_values(key_of[8], (REQS, QLEN, D), 0.1, 0.59765625, ((0, 64), (2, 4))),
        "out_weight": normal_values(key_of[9], (QH * HD, D), HD ** -0.5, 0.5, ((0, 4),)),
    }


masked_score = -1e+30

def block_attend(query_rows, key_rows, value_rows, visible):
    batch_size, row_count, query_width = query_rows.shape
    key_span = key_rows.shape[1]
    key_heads = key_rows.shape[2] // HD
    group_width = query_width // HD // key_heads
    query_split = query_rows.astype(jnp.float32).reshape(batch_size, row_count, key_heads, group_width, HD)
    key_split = key_rows.astype(jnp.float32).reshape(batch_size, key_span, key_heads, HD)
    value_split = value_rows.astype(jnp.float32).reshape(batch_size, key_span, key_heads, HD)
    scores = jnp.einsum('blkge,bske->bkgls', query_split, key_split) * (1.0 / math.sqrt(HD))
    if visible is not None:
        scores = jnp.where(visible, scores, masked_score)
    maxima = lax.optimization_barrier(jnp.max(scores, axis=-1, keepdims=True))
    exponent = jnp.exp(scores - maxima)
    totals = lax.optimization_barrier(jnp.sum(exponent, axis=-1, keepdims=True))
    weights = exponent.astype(jnp.bfloat16)
    numerator = jnp.einsum('bkgls,bske->blkge', weights.astype(jnp.float32), value_split)
    divisor = jnp.transpose(totals, (0, 3, 1, 2, 4))
    normed = (numerator / divisor).astype(jnp.bfloat16).reshape(batch_size, row_count, query_width)
    log_total = (maxima + jnp.log(totals))[..., 0].reshape(batch_size, key_heads * group_width, row_count)
    return (normed, log_total)

def merge_blocks(block_parts, block_logs, length):
    block_count, head_count, row_count = block_logs.shape
    ceiling = lax.optimization_barrier(jnp.max(block_logs, axis=0, keepdims=True))
    factors = jnp.exp(block_logs - ceiling)
    spread = jnp.transpose(factors, (0, 2, 1))[:, :, :, None]
    stacked = block_parts.reshape(block_count, row_count, head_count, -1)
    combined = lax.optimization_barrier(jnp.sum(spread * stacked, axis=0)) / lax.optimization_barrier(jnp.sum(spread, axis=0))
    live_rows = jnp.arange(row_count)[:, None] < length
    return jnp.where(live_rows, combined.reshape(row_count, -1), 0.0).astype(jnp.bfloat16)

def reference(queries, own_keys, own_values, passage_keys, passage_values, passage_slot, picks, lengths, residual, out_weight):
    row_count = queries.shape[1]
    visible = jnp.arange(row_count)[None, :] <= jnp.arange(row_count)[:, None]

    def one_request(packed):
        query_tile, key_tile, value_tile, pick_row, length, residual_tile = packed
        stored_rows = passage_slot[pick_row]
        tiled_queries = jnp.broadcast_to(query_tile[None], (PICKS,) + query_tile.shape)
        block_parts, block_logs = block_attend(tiled_queries, passage_keys[stored_rows], passage_values[stored_rows], None)
        own_part, own_log = block_attend(query_tile[None], key_tile[None], value_tile[None], visible)
        all_parts = jnp.concatenate([block_parts.astype(jnp.float32), own_part.astype(jnp.float32)], axis=0)
        all_logs = jnp.concatenate([block_logs, own_log], axis=0)
        attended = merge_blocks(all_parts, all_logs, length)
        projected = jnp.dot(attended, out_weight, preferred_element_type=jnp.float32)
        return (residual_tile.astype(jnp.float32) + projected).astype(jnp.bfloat16)
    return lax.map(one_request, (queries, own_keys, own_values, picks, lengths, residual))
```

```python
import math

import jax
import jax.numpy as jnp
import numpy as np
from jax import lax
from jax.experimental import pallas as pl
from jax.experimental.pallas import tpu as pltpu
from jax.sharding import Mesh, PartitionSpec as P

HD = 128
PICKS = 16
PASS_DEV = 16
ROWS = 256
WIDE = 2 * ROWS
SCALE = 1.0 / math.sqrt(HD)
EXP2_SCALE = SCALE * math.log2(math.e)
EMPTY = -1e30
XS, ZS = 4, 8
REQS_CORE = XS * ZS
bf16, f32 = jnp.bfloat16, jnp.float32


def dot(a, b, dims=((1,), (0,))):
    return lax.dot_general(a, b, (dims, ((), ())), preferred_element_type=f32)


def chunk_attend(keys, values, queries, visible=None):
    scores = dot(keys, queries)
    if visible is not None:
        scores = jnp.where(visible, scores, EMPTY)
    top = jnp.max(scores, axis=0, keepdims=True)
    e = jnp.exp2((scores - top) * EXP2_SCALE)
    den = jnp.sum(e, axis=0, keepdims=True)
    out = dot(values, e.astype(bf16), ((0,), (0,)))
    part = (out / den).astype(bf16).astype(f32)
    return part, top * SCALE + jnp.log(den)


def merge(acc_a, lse_a, acc_b, lse_b):
    top = jnp.maximum(lse_a, lse_b)
    wa, wb = jnp.exp(lse_a - top), jnp.exp(lse_b - top)
    den = wa + wb
    return acc_a * (wa / den) + acc_b * (wb / den), top + jnp.log(den)


def attend_kernel(groups, meta, *refs):
    m = len(groups)
    ins = refs[:m]
    kown, vown, ksib, vsib = refs[m : m + 4]
    accs, lses = refs[m + 4 : 2 * m + 4], refs[2 * m + 4 : 3 * m + 4]
    qbuf, kbuf, vbuf, acc_s, lse_s, items, qsem, ksem, vsem = refs[3 * m + 4 :]
    offs = np.cumsum([0] + [len(g) for g in groups])

    def q_copy(i):
        return pltpu.make_async_copy(
            ins[i], qbuf.at[pl.ds(int(offs[i]), len(groups[i]))], qsem.at[i]
        )

    for i in range(m):
        q_copy(i).start()

    x, z = meta[4 * REQS_CORE], meta[4 * REQS_CORE + 1]
    count = jnp.int32(0)
    for i, group in enumerate(groups):
        for j, (dx, dz) in enumerate(group):
            b = int(offs[i]) + j
            r = ((x + dx) & (XS - 1)) * ZS + ((z + dz) & (ZS - 1))
            s0, s1 = meta[4 * r], meta[4 * r + 1]
            big = (meta[4 * r + 2] > ROWS // 2).astype(jnp.int32)
            has0, has1 = (s0 >= 0).astype(jnp.int32), (s1 >= 0).astype(jnp.int32)
            items[count] = b + (s0 << 9) + (1 << 16) + ((1 - has1) << 17) + (big << 18)
            count = count + has0
            items[count] = b + (1 << 8) + (s1 << 9) + ((1 - has0) << 16) + (1 << 17) + (big << 18)
            count = count + has1

            @pl.when(has0 + has1 == 0)
            def _():
                accs[i][j] = jnp.zeros((HD, WIDE), bf16)
                lses[i][j] = jnp.full((1, WIDE), EMPTY, f32)

    def kv_start(n, buf):
        code = items[n]
        slot = (code >> 9) & (PASS_DEV - 1)
        sibling = (code >> 8) & 1

        @pl.when(sibling == 0)
        def _():
            pltpu.make_async_copy(kown.at[slot], kbuf.at[buf], ksem.at[buf]).start()
            pltpu.make_async_copy(vown.at[slot], vbuf.at[buf], vsem.at[buf]).start()

        @pl.when(sibling == 1)
        def _():
            pltpu.make_async_copy(ksib.at[slot], kbuf.at[buf], ksem.at[buf]).start()
            pltpu.make_async_copy(vsib.at[slot], vbuf.at[buf], vsem.at[buf]).start()

    @pl.when(count > 0)
    def _():
        kv_start(0, 0)

    for i in range(m):
        q_copy(i).wait()

    def put(first, lanes, part, lse):
        @pl.when(first == 1)
        def _():
            for at, of in lanes:
                acc_s[:, at] = part[:, of]
                lse_s[:, at] = lse[:, of]

        @pl.when(first == 0)
        def _():
            for at, of in lanes:
                acc_s[:, at], lse_s[:, at] = merge(
                    acc_s[:, at], lse_s[:, at], part[:, of], lse[:, of]
                )

    def step(n, carry):
        buf = n % 2

        @pl.when(n + 1 < count)
        def _():
            kv_start(n + 1, 1 - buf)

        pltpu.make_async_copy(kown.at[0], kbuf.at[buf], ksem.at[buf]).wait()
        pltpu.make_async_copy(vown.at[0], vbuf.at[buf], vsem.at[buf]).wait()
        code = items[n]
        b = code & 255
        first, last, big = (code >> 16) & 1, (code >> 17) & 1, (code >> 18) & 1
        half = ROWS // 2

        @pl.when(big == 1)
        def _():
            done = [
                chunk_attend(kbuf[buf], vbuf[buf], qbuf[b, :, h * ROWS : (h + 1) * ROWS])
                for h in range(2)
            ]
            for h in range(2):
                put(first, [(slice(h * ROWS, (h + 1) * ROWS), slice(0, ROWS))], *done[h])

        @pl.when(big == 0)
        def _():
            q = jnp.concatenate([qbuf[b, :, :half], qbuf[b, :, ROWS : ROWS + half]], axis=1)
            part, lse = chunk_attend(kbuf[buf], vbuf[buf], q)
            put(
                first,
                [(slice(0, half), slice(0, half)), (slice(ROWS, ROWS + half), slice(half, ROWS))],
                part,
                lse,
            )
            for h in range(2):
                rest = slice(h * ROWS + half, (h + 1) * ROWS)
                acc_s[:, rest] = jnp.zeros((HD, half), f32)
                lse_s[:, rest] = jnp.full((1, half), EMPTY, f32)

        for i, group in enumerate(groups):
            lo = int(offs[i])

            @pl.when((last == 1) & (b >= lo) & (b < lo + len(group)))
            def _():
                accs[i][b - lo] = acc_s[...].astype(bf16)
                lses[i][b - lo] = lse_s[...]

        return carry

    lax.fori_loop(0, count, step, 0)


def attend(meta, arrays, groups, kv):
    total = sum(len(g) for g in groups)
    m = len(groups)
    any_spec = pl.BlockSpec(memory_space=pl.ANY)
    vmem = pl.BlockSpec(memory_space=pltpu.VMEM)
    outs = pl.pallas_call(
        lambda *refs: attend_kernel(groups, *refs),
        out_shape=[jax.ShapeDtypeStruct((len(g), HD, WIDE), bf16) for g in groups]
        + [jax.ShapeDtypeStruct((len(g), 1, WIDE), f32) for g in groups],
        in_specs=[pl.BlockSpec(memory_space=pltpu.SMEM)] + [any_spec] * (m + 4),
        out_specs=[vmem] * (2 * m),
        scratch_shapes=[
            pltpu.VMEM((total, HD, WIDE), bf16),
            pltpu.VMEM((2, 512, HD), bf16),
            pltpu.VMEM((2, 512, HD), bf16),
            pltpu.VMEM((HD, WIDE), f32),
            pltpu.VMEM((1, WIDE), f32),
            pltpu.SMEM((2 * total + 2,), jnp.int32),
            pltpu.SemaphoreType.DMA((m,)),
            pltpu.SemaphoreType.DMA((2,)),
            pltpu.SemaphoreType.DMA((2,)),
        ],
        compiler_params=pltpu.CompilerParams(vmem_limit_bytes=40 * 2**20),
        cost_estimate=pl.CostEstimate(
            flops=total * 4 * 512 * HD * WIDE,
            bytes_accessed=total * 2**19,
            transcendentals=total * 512 * WIDE,
        ),
        name="attend",
    )(meta, *arrays, *kv)
    return list(zip(outs[:m], outs[m:]))


def own_kernel(qa, qb, k, v, acc_a, acc_b, lse_a, lse_b):
    key = lax.broadcasted_iota(jnp.int32, (ROWS, ROWS), 0)
    row = lax.broadcasted_iota(jnp.int32, (ROWS, ROWS), 1)
    for q, acc, lse in ((qa, acc_a, lse_a), (qb, acc_b, lse_b)):
        for h in range(2):
            at = slice(h * ROWS, (h + 1) * ROWS)
            acc[0, :, at], lse[0, :, at] = chunk_attend(k[...], v[...], q[0, :, at], key <= row)


def own_attend(qa, qb, k, v):
    vmem = pl.BlockSpec(memory_space=pltpu.VMEM)
    acc_a, acc_b, lse_a, lse_b = pl.pallas_call(
        own_kernel,
        out_shape=[jax.ShapeDtypeStruct((1, HD, WIDE), f32)] * 2
        + [jax.ShapeDtypeStruct((1, 1, WIDE), f32)] * 2,
        in_specs=[vmem] * 4,
        out_specs=[vmem] * 4,
        compiler_params=pltpu.CompilerParams(vmem_limit_bytes=32 * 2**20),
        name="own_attend",
    )(qa, qb, k, v)
    return (acc_a, lse_a), (acc_b, lse_b)


def shift(value, axis, by):
    n = lax.axis_size(axis)
    pairs = [(i, (i + by) % n) for i in range(n)]
    return jax.tree.map(lambda leaf: lax.ppermute(leaf, axis, pairs), value)


def join(mine, came):
    acc, lse = merge(mine[0].astype(f32), mine[1], came[0].astype(f32), came[1])
    return acc.astype(bf16), lse


def join_f32(*parts):
    top = parts[0][1]
    for _, lse in parts[1:]:
        top = jnp.maximum(top, lse)
    weights = [jnp.exp(lse - top) for _, lse in parts]
    den = sum(weights)
    acc = sum(part.astype(f32) * w for (part, _), w in zip(parts, weights)) / den
    return acc, top + jnp.log(den)


def cut(pair, blocks=slice(None), lanes=slice(None)):
    return pair[0][blocks, :, lanes], pair[1][blocks, :, lanes]


def on_device(
    queries,
    own_keys,
    own_values,
    passage_keys,
    passage_values,
    passage_slot,
    picks,
    lengths,
    residual,
    out_weight,
):
    x, z, core, t = (lax.axis_index(a) for a in ("x", "z", "core", "tensor"))
    head0, head1 = slice(0, ROWS), slice(ROWS, WIDE)

    turned = queries[0].reshape(ROWS, 4, HD).transpose(2, 1, 0).reshape(1, HD, 4 * ROWS)
    qa, qb = turned[:, :, :WIDE], turned[:, :, WIDE:]

    a_r, a_l = shift(qa, "x", 1), shift(qa, "x", -1)
    a_d = jnp.concatenate(
        [shift(a_r[:, :, head0], "x", 1), shift(a_l[:, :, head1], "x", -1)], axis=2
    )
    lo = [jnp.concatenate([qa, a_r], axis=0)]
    hi = [jnp.concatenate([a_l, a_d], axis=0)]
    lo_up, lo_dn, hi_up, hi_dn = list(lo), list(lo), list(hi), list(hi)

    b_up, b_dn = [qb], [qb]
    for _ in range(3):
        b_up.append(shift(b_up[-1], "z", 1))
        b_dn.append(shift(b_dn[-1], "z", -1))
    b_far = jnp.concatenate(
        [shift(b_up[3][:, :, head0], "z", 1), shift(b_dn[3][:, :, head1], "z", -1)], axis=2
    )
    b_lo = jnp.concatenate([qb, b_up[1], b_dn[1], b_up[2]], axis=0)
    b_hi = jnp.concatenate([b_dn[2], b_up[3], b_dn[3], b_far], axis=0)

    for k in range(4):
        lo_up.append(shift(lo_up[-1], "z", 1))
        hi_dn.append(shift(hi_dn[-1], "z", -1))
        if k < 3:
            lo_dn.append(shift(lo_dn[-1], "z", -1))
            hi_up.append(shift(hi_up[-1], "z", 1))

    br_lo, br_hi = shift(b_lo, "x", 1), shift(b_hi, "x", 1)
    bl_lo, bl_hi = shift(b_lo, "x", -1), shift(b_hi, "x", -1)
    b2_lo, b2_hi = shift(br_lo, "x", 1), shift(bl_hi, "x", -1)

    keys_sib, values_sib = shift((passage_keys, passage_values), "core", 1)
    kv = (passage_keys, passage_values, keys_sib, values_sib)

    storage = jnp.sum(
        jnp.where(
            picks[0][:, None] == jnp.arange(passage_slot.shape[0], dtype=jnp.int32)[None, :],
            passage_slot[None, :],
            0,
        ),
        axis=1,
    )
    told = jnp.concatenate([storage, lengths, jnp.zeros((15,), jnp.int32)])[None, :]
    told = lax.all_gather(told, ("x", "z", "core"), axis=0, tiled=True)
    told = lax.dynamic_index_in_dim(told.reshape(REQS_CORE, 2, 32), core, 1, keepdims=False)
    rows, spans = told[:, :PICKS], told[:, PICKS]
    chip = (x * ZS + z) * 2
    slot0 = jnp.max(jnp.where(rows // PASS_DEV == chip + core, rows % PASS_DEV, -1), axis=1)
    slot1 = jnp.max(jnp.where(rows // PASS_DEV == chip + 1 - core, rows % PASS_DEV, -1), axis=1)
    table = jnp.stack([slot0, slot1, spans, spans], axis=1).reshape(-1)
    place = jnp.stack([x, z, x, z, x, z, x, z]).astype(jnp.int32)
    meta = jnp.concatenate([table, place])

    columns = out_weight.shape[1] // 4

    def weight_for(by):
        start = ((t + by) & 3) * columns
        return lax.dynamic_slice_in_dim(out_weight, start, columns, axis=1)

    weights = [weight_for(0)] + [shift(weight_for(by), "tensor", by) for by in (1, 3, 2)]

    own_a, own_b = own_attend(qa, qb, own_keys[0], own_values[0])

    lo_x, hi_x = (0, -1), (1, 2)

    def lo_at(dz):
        return [(dx, dz) for dx in lo_x]

    def hi_at(dz):
        return [(dx, dz) for dx in hi_x]

    pa = {}
    pa["lo", 0], pa["hi", 0] = attend(meta, [lo[0], hi[0]], [lo_at(0), hi_at(0)], kv)
    b_lo_z, b_hi_z = (0, -1, 1, -2), (2, -3, 3, 4)

    def b_at(dx, zs):
        return [(dx, dz) for dz in zs]

    pb_lo, pb_hi = attend(meta, [b_lo, b_hi], [b_at(0, b_lo_z), b_at(0, b_hi_z)], kv)
    for k in range(1, 4):
        pa["lo", -k], pa["hi", -k], pa["lo", k], pa["hi", k] = attend(
            meta,
            [lo_up[k], hi_up[k], lo_dn[k], hi_dn[k]],
            [lo_at(-k), hi_at(-k), lo_at(k), hi_at(k)],
            kv,
        )
    pbr_lo, pbr_hi, pbl_lo, pbl_hi = attend(
        meta,
        [br_lo, br_hi, bl_lo, bl_hi],
        [b_at(-1, b_lo_z), b_at(-1, b_hi_z), b_at(1, b_lo_z), b_at(1, b_hi_z)],
        kv,
    )
    pa["lo", 4], pa["hi", 4], pb2_lo, pb2_hi = attend(
        meta,
        [lo_up[4], hi_dn[4], b2_lo, b2_hi],
        [lo_at(4), hi_at(4), b_at(2, b_lo_z), b_at(2, b_hi_z)],
        kv,
    )

    def back(start, stops, axis, by):
        moving = start
        for stop in stops:
            moving = join(stop, shift(moving, axis, by))
        return moving

    a_lo_up = shift(back(pa["lo", 4], [pa["lo", -3], pa["lo", -2], pa["lo", -1]], "z", -1), "z", -1)
    a_hi_up = shift(back(pa["hi", -3], [pa["hi", -2], pa["hi", -1]], "z", -1), "z", -1)
    a_lo_dn = shift(back(pa["lo", 3], [pa["lo", 2], pa["lo", 1]], "z", 1), "z", 1)
    a_hi_dn = shift(back(pa["hi", 4], [pa["hi", 3], pa["hi", 2], pa["hi", 1]], "z", 1), "z", 1)
    sum_lo = join_f32(pa["lo", 0], a_lo_up, a_lo_dn)
    sum_hi = join_f32(pa["hi", 0], a_hi_up, a_hi_dn)
    a_own, a_from_r = cut(sum_lo, slice(0, 1)), cut(sum_lo, slice(1, 2))
    a_from_l, a_far = cut(sum_hi, slice(0, 1)), cut(sum_hi, slice(1, 2))

    def narrow(pair):
        return pair[0].astype(bf16), pair[1]

    def beside(first, second):
        return tuple(jnp.concatenate(p, axis=2) for p in zip(first, second))

    far_r = join(cut(a_from_r, lanes=head0), shift(narrow(cut(a_far, lanes=head0)), "x", -1))
    far_l = join(cut(a_from_l, lanes=head1), shift(narrow(cut(a_far, lanes=head1)), "x", 1))
    got_r = shift(beside(far_r, narrow(cut(a_from_r, lanes=head1))), "x", -1)
    got_l = shift(beside(narrow(cut(a_from_l, lanes=head0)), far_l), "x", 1)
    done_a, _ = join_f32(a_own, got_r, got_l, own_a)

    b_r_lo = shift(join(pbr_lo, shift(pb2_lo, "x", -1)), "x", -1)
    b_r_hi = shift(pbr_hi, "x", -1)
    b_l_lo = shift(pbl_lo, "x", 1)
    b_l_hi = shift(join(pbl_hi, shift(pb2_hi, "x", 1)), "x", 1)
    tot_lo = join_f32(pb_lo, b_r_lo, b_l_lo)
    tot_hi = join_f32(pb_hi, b_r_hi, b_l_hi)
    at_z = {}
    for n, dz in enumerate(b_lo_z):
        at_z[dz] = cut(tot_lo, slice(n, n + 1))
    for n, dz in enumerate(b_hi_z):
        at_z[dz] = cut(tot_hi, slice(n, n + 1))
    up = join(cut(at_z[-3], lanes=head0), shift(narrow(cut(at_z[4], lanes=head0)), "z", -1))
    up = beside(up, narrow(cut(at_z[-3], lanes=head1)))
    dn = join(cut(at_z[3], lanes=head1), shift(narrow(cut(at_z[4], lanes=head1)), "z", 1))
    dn = beside(narrow(cut(at_z[3], lanes=head0)), dn)
    up = shift(back(up, [at_z[-2], at_z[-1]], "z", -1), "z", -1)
    dn = shift(back(dn, [at_z[2], at_z[1]], "z", 1), "z", 1)
    done_b, _ = join_f32(at_z[0], up, dn, own_b)

    live = (jnp.arange(WIDE) & (ROWS - 1)) < lengths[0]
    done = jnp.concatenate([done_a, done_b], axis=0)
    done = jnp.where(live[None, None, :], done, 0.0).astype(bf16)
    attended = done.reshape(2, HD, 2, ROWS).transpose(3, 0, 2, 1).reshape(ROWS, 4 * HD)

    others = [shift(attended, "tensor", by) for by in (1, 3, 2)]
    total = residual[0].astype(f32)
    for block, weight in zip([attended] + others, weights):
        total = total + dot(block, weight)
    return total.astype(bf16)[None]


def solution(mesh):
    grid = Mesh(mesh.devices.reshape(XS, ZS, 2, 4), ("x", "z", "core", "tensor"))
    cache = ("x", "z", "core")
    in_specs = (
        P(cache, None, "tensor"),
        P(cache, None, "tensor"),
        P(cache, None, "tensor"),
        P(cache, None, "tensor"),
        P(cache, None, "tensor"),
        P(),
        P(cache, None),
        P(cache),
        P(cache, None, "tensor"),
        P("tensor", None),
    )
    return jax.shard_map(
        on_device,
        mesh=grid,
        in_specs=in_specs,
        out_specs=P(cache, None, "tensor"),
        check_vma=False,
    )
```

```python
import math

import jax
import jax.numpy as jnp
from jax import lax
from jax.experimental import pallas as pl
from jax.experimental.pallas import tpu as pltpu
from jax.sharding import Mesh, PartitionSpec as P

HD = 128
PICKS = 16
PASS_DEV = 16
PLEN = 512
ROWS = 256
WIDE = 2 * ROWS
LANES = 128
DEPTH = 4
A_ORDER = (0, -1, 1, 2)
SCALE = 1.0 / math.sqrt(HD)
EXP2_SCALE = SCALE * math.log2(math.e)
EMPTY = -1e30
XS, ZS = 4, 8
REQS_CORE = XS * ZS
TAIL = 32
ONE = HD + 16
bf16, f32 = jnp.bfloat16, jnp.float32
VMEM = pl.BlockSpec(memory_space=pltpu.VMEM)
SMEM = pl.BlockSpec(memory_space=pltpu.SMEM)
ANY = pl.BlockSpec(memory_space=pl.ANY)


def dot(a, b):
    return lax.dot_general(a, b, (((1,), (0,)), ((), ())), preferred_element_type=f32)


def chunk_attend(keys, values_t, queries, visible=None):
    scores = dot(keys, queries)
    if visible is not None:
        scores = jnp.where(visible, scores, EMPTY)
    top = jnp.max(scores, axis=0, keepdims=True)
    e = jnp.exp2((scores - top) * EXP2_SCALE)
    den = jnp.sum(e, axis=0, keepdims=True)
    part = (dot(values_t, e.astype(bf16)) / den).astype(bf16).astype(f32)
    return part, top * SCALE + jnp.log(den)


def weigh(lses):
    top = lses[0]
    for lse in lses[1:]:
        top = jnp.maximum(top, lse)
    weights = [jnp.exp(lse - top) for lse in lses]
    den = weights[0]
    for w in weights[1:]:
        den = den + w
    return [w / den for w in weights], top + jnp.log(den)


def split3(lse):
    hi = lse.astype(bf16).astype(f32)
    mid = (lse - hi).astype(bf16).astype(f32)
    return hi, mid, lse - hi - mid


def message(n):
    return jax.ShapeDtypeStruct((n * HD + TAIL, WIDE), bf16)


def blocks_in(ref):
    return (ref.shape[0] - TAIL) // HD


def block_at(ref, b):
    return ref[b * HD : (b + 1) * HD, :].astype(f32)


def lse_in(ref):
    n = blocks_in(ref) * HD
    tail = ref[n : n + TAIL, :].astype(f32)
    return tail[0:8] + tail[8:16] + tail[16:24]


def put_lse(ref, lse):
    n = blocks_in(ref) * HD
    tail = jnp.concatenate([*split3(lse), jnp.zeros_like(lse)], axis=0)
    ref[n : n + TAIL, :] = tail.astype(bf16)


def attend_kernel(groups, meta, *refs):
    m = len(groups)
    ins = refs[:m]
    kv_own, kv_sib = refs[m : m + 2]
    outs = refs[m + 2 : 2 * m + 2]
    qbuf, kvbuf, acc_s, lse_s, items, qsem, kvsem = refs[2 * m + 2 :]
    offs = [sum(len(g) for g in groups[:i]) for i in range(m)]

    def q_copy(i):
        return pltpu.make_async_copy(
            ins[i], qbuf.at[pl.ds(offs[i], len(groups[i]))], qsem.at[i]
        )

    for i in range(m):
        q_copy(i).start()

    x, z = meta[4 * REQS_CORE], meta[4 * REQS_CORE + 1]
    count = jnp.int32(0)
    for i, group in enumerate(groups):
        for j, request in enumerate(group):
            r = request(x, z)
            s0, s1 = meta[4 * r], meta[4 * r + 1]
            big = (meta[4 * r + 2] > ROWS // 2).astype(jnp.int32)
            kind = (s0 >= 0).astype(jnp.int32) + 2 * (s1 >= 0).astype(jnp.int32)
            items[count] = (
                (offs[i] + j)
                + ((s0 & 15) << 8)
                + ((s1 & 15) << 12)
                + (kind << 16)
                + (big << 18)
                + ((8 * i + j) << 20)
            )
            count = count + (kind > 0).astype(jnp.int32)

            @pl.when(kind == 0)
            def _():
                outs[i][j * HD : (j + 1) * HD, :] = jnp.zeros((HD, WIDE), bf16)

    lse_s[...] = jnp.full(lse_s.shape, EMPTY, f32)

    def kv_copy(ref, slot, buf, pos):
        return pltpu.make_async_copy(ref.at[slot], kvbuf.at[buf, pos], kvsem.at[buf, pos])

    def kv_start(n, buf):
        code = items[n]
        s0, s1, kind = (code >> 8) & 15, (code >> 12) & 15, (code >> 16) & 3

        @pl.when(kind != 2)
        def _():
            kv_copy(kv_own, s0, buf, 0).start()

        @pl.when(kind == 2)
        def _():
            kv_copy(kv_sib, s1, buf, 0).start()

        @pl.when(kind == 3)
        def _():
            kv_copy(kv_sib, s1, buf, 1).start()

    for ahead in range(DEPTH - 1):

        @pl.when(count > ahead)
        def _():
            kv_start(ahead, ahead)

    for i in range(m):
        q_copy(i).wait()

    def step(n, carry):
        buf = n & (DEPTH - 1)

        @pl.when(n + DEPTH - 1 < count)
        def _():
            kv_start(n + DEPTH - 1, (n + DEPTH - 1) & (DEPTH - 1))

        code = items[n]
        b = code & 255
        kind, big, row = (code >> 16) & 3, (code >> 18) & 1, code >> 20

        kv_copy(kv_own, 0, buf, 0).wait()

        @pl.when(kind == 3)
        def _():
            kv_copy(kv_sib, 0, buf, 1).wait()

        def work(picked, starts):
            done = []
            for pos in range(picked):
                keys, values_t = kvbuf[buf, pos, 0], kvbuf[buf, pos, 1].T
                done.append(
                    [chunk_attend(keys, values_t, qbuf[b, :, s : s + LANES]) for s in starts]
                )
            for n_s, s in enumerate(starts):
                if picked == 1:
                    acc, lse = done[0][n_s]
                else:
                    (p0, l0), (p1, l1) = done[0][n_s], done[1][n_s]
                    (w0, w1), lse = weigh([l0, l1])
                    acc = p0 * w0 + p1 * w1
                acc_s[:, s : s + LANES] = acc.astype(bf16)
                lse_s[row, :, s : s + LANES] = lse

        full, short = (0, 128, 256, 384), (0, 256)
        for picked, is_kind in ((1, kind != 3), (2, kind == 3)):

            @pl.when((big == 1) & is_kind)
            def _():
                work(picked, full)

            @pl.when((big == 0) & is_kind)
            def _():
                work(picked, short)
                for s in (128, 384):
                    acc_s[:, s : s + LANES] = jnp.zeros((HD, LANES), bf16)

        for i, group in enumerate(groups):

            @pl.when((b >= offs[i]) & (b < offs[i] + len(group)))
            def _():
                at = pl.multiple_of((b - offs[i]) * HD, HD)
                outs[i][pl.ds(at, HD), :] = acc_s[...]

        return carry

    lax.fori_loop(0, count, step, 0)
    for i in range(m):
        put_lse(outs[i], jnp.concatenate([lse_s[8 * i + j] for j in range(8)], axis=0))


def attend(meta, arrays, groups, kv):
    total = sum(len(g) for g in groups)
    m = len(groups)
    return pl.pallas_call(
        lambda *refs: attend_kernel(groups, *refs),
        out_shape=[message(len(g)) for g in groups],
        in_specs=[SMEM] + [ANY] * (m + 2),
        out_specs=[VMEM] * m,
        scratch_shapes=[
            pltpu.VMEM((total, HD, WIDE), bf16),
            pltpu.VMEM((DEPTH, 2, 2, PLEN, HD), bf16),
            pltpu.VMEM((HD, WIDE), bf16),
            pltpu.VMEM((8 * m, 1, WIDE), f32),
            pltpu.SMEM((total + 1,), jnp.int32),
            pltpu.SemaphoreType.DMA((m,)),
            pltpu.SemaphoreType.DMA((DEPTH, 2)),
        ],
        compiler_params=pltpu.CompilerParams(vmem_limit_bytes=40 * 2**20),
        cost_estimate=pl.CostEstimate(
            flops=total * 4 * PLEN * HD * WIDE,
            bytes_accessed=total * 2**19,
            transcendentals=total * PLEN * WIDE,
        ),
        name="attend",
    )(meta, *arrays, *kv)


def own_kernel(qa, qb, k, v, acc_a, acc_b, lse_a, lse_b):
    key = lax.broadcasted_iota(jnp.int32, (ROWS, LANES), 0)
    row = lax.broadcasted_iota(jnp.int32, (ROWS, LANES), 1)
    keys, values_t = k[...], v[...].T
    for q, acc, lse in ((qa, acc_a, lse_a), (qb, acc_b, lse_b)):
        for s in range(0, WIDE, LANES):
            at = slice(s, s + LANES)
            acc[:, at], lse[:, at] = chunk_attend(
                keys, values_t, q[:, at], key <= row + (s & (ROWS - 1))
            )


def own_attend(qa, qb, k, v):
    acc_a, acc_b, lse_a, lse_b = pl.pallas_call(
        own_kernel,
        out_shape=[jax.ShapeDtypeStruct((HD, WIDE), f32)] * 2
        + [jax.ShapeDtypeStruct((1, WIDE), f32)] * 2,
        in_specs=[VMEM] * 4,
        out_specs=[VMEM] * 4,
        compiler_params=pltpu.CompilerParams(vmem_limit_bytes=32 * 2**20),
        name="own_attend",
    )(qa, qb, k, v)
    return (acc_a, lse_a), (acc_b, lse_b)


def join_kernel(firsts, *refs):
    n = len(firsts)
    for i, first in enumerate(firsts):
        mine, came, out = refs[2 * i], refs[2 * i + 1], refs[2 * n + i]
        count = blocks_in(came)
        lse_m, lse_c = lse_in(mine), lse_in(came)
        if first:
            lse_c = jnp.concatenate(
                [jnp.full((first, WIDE), EMPTY, f32), lse_c[: 8 - first]], axis=0
            )
        (wm, wc), lse = weigh([lse_m, lse_c])
        for b in range(blocks_in(mine)):
            if first <= b < first + count:
                acc = block_at(mine, b) * wm[b : b + 1] + block_at(came, b - first) * wc[b : b + 1]
                out[b * HD : (b + 1) * HD, :] = acc.astype(bf16)
            else:
                out[b * HD : (b + 1) * HD, :] = mine[b * HD : (b + 1) * HD, :]
        put_lse(out, lse)


def join(*triples):
    return pl.pallas_call(
        lambda *refs: join_kernel([t[2] for t in triples], *refs),
        out_shape=[jax.ShapeDtypeStruct(t[0].shape, bf16) for t in triples],
        in_specs=[VMEM] * (2 * len(triples)),
        out_specs=[VMEM] * len(triples),
        compiler_params=pltpu.CompilerParams(vmem_limit_bytes=32 * 2**20),
        name="join",
    )(*[a for t in triples for a in t[:2]])


def gather_kernel(turned, meta, a, b, c, out):
    weights, lse = weigh([lse_in(a), lse_in(b), lse_in(c)])
    x = meta[4 * REQS_CORE] if turned else 0
    parts = split3(lse)
    for n in range(blocks_in(a)):
        acc = sum(block_at(ref, n) * w[n : n + 1] for ref, w in zip((a, b, c), weights))
        at = (x + A_ORDER[n]) & (XS - 1) if turned else n
        out[at, :HD, :] = acc.astype(bf16)
        tail = [p[n : n + 1] for p in parts] + [jnp.zeros((13, WIDE), f32)]
        out[at, HD:, :] = jnp.concatenate(tail, axis=0).astype(bf16)


def gather(meta, a, b, c, turned):
    n = (a.shape[0] - TAIL) // HD
    return pl.pallas_call(
        lambda *refs: gather_kernel(turned, *refs),
        out_shape=jax.ShapeDtypeStruct((n, ONE, WIDE), bf16),
        in_specs=[SMEM] + [VMEM] * 3,
        out_specs=VMEM,
        compiler_params=pltpu.CompilerParams(vmem_limit_bytes=32 * 2**20),
        name="gather",
    )(meta, a, b, c)


def finish_kernel(length, came, acc_own, lse_own, out):
    n = came.shape[0]
    lses = [lse_own[...]]
    for i in range(n):
        tail = came[i, HD:, :].astype(f32)
        lses.append(tail[0:1] + tail[1:2] + tail[2:3])
    weights, _ = weigh(lses)
    acc = acc_own[...] * weights[0]
    for i in range(n):
        acc = acc + came[i, :HD, :].astype(f32) * weights[i + 1]
    row = lax.broadcasted_iota(jnp.int32, (HD, WIDE), 1) & (ROWS - 1)
    acc = jnp.where(row < length[0], acc, 0.0)
    for h in range(2):
        out[:, h * HD : (h + 1) * HD] = acc[:, h * ROWS : (h + 1) * ROWS].T.astype(bf16)


def finish(length, came, own):
    return pl.pallas_call(
        finish_kernel,
        out_shape=jax.ShapeDtypeStruct((ROWS, 2 * HD), bf16),
        in_specs=[SMEM, VMEM, VMEM, VMEM],
        out_specs=VMEM,
        compiler_params=pltpu.CompilerParams(vmem_limit_bytes=32 * 2**20),
        name="finish",
    )(length, came, *own)


def shift(value, axis, by):
    n = lax.axis_size(axis)
    return lax.ppermute(value, axis, [(i, (i + by) % n) for i in range(n)])


def on_device(
    queries,
    own_keys,
    own_values,
    passage_keys,
    passage_values,
    passage_slot,
    picks,
    lengths,
    residual,
    out_weight,
):
    x, z, core, t = (lax.axis_index(a) for a in ("x", "z", "core", "tensor"))

    turned = queries[0].reshape(ROWS, 4, HD).transpose(2, 1, 0).reshape(HD, 4 * ROWS)
    qa, qb = turned[:, :WIDE], turned[:, WIDE:]

    storage = jnp.sum(
        jnp.where(
            picks[0][:, None] == jnp.arange(passage_slot.shape[0], dtype=jnp.int32)[None, :],
            passage_slot[None, :],
            0,
        ),
        axis=1,
    )
    told = jnp.concatenate([storage, lengths, jnp.zeros((15,), jnp.int32)])
    a_r, a_l = shift(qa, "x", 1), shift(qa, "x", -1)
    told = lax.all_to_all(
        jnp.broadcast_to(told[None, :], (REQS_CORE, 32)),
        ("x", "z"),
        split_axis=0,
        concat_axis=0,
        tiled=True,
    )
    rows, spans = told[:, :PICKS], told[:, PICKS]
    chip = (x * ZS + z) * 2
    slot0 = jnp.max(jnp.where(rows // PASS_DEV == chip + core, rows % PASS_DEV, -1), axis=1)
    slot1 = jnp.max(jnp.where(rows // PASS_DEV == chip + 1 - core, rows % PASS_DEV, -1), axis=1)
    table = jnp.stack([slot0, slot1, spans, spans], axis=1).reshape(-1)
    place = jnp.stack([x, z, x, z, x, z, x, z]).astype(jnp.int32)
    meta = jnp.concatenate([table, place])
    kv_own = jnp.stack([passage_keys, passage_values], axis=1)
    kv = (kv_own, shift(kv_own, "core", 1))
    a_r, a_l, meta, kv = lax.optimization_barrier((a_r, a_l, meta, kv))


    columns = out_weight.shape[1] // 4

    def weight_for(by):
        start = ((t + by) & 3) * columns
        return lax.dynamic_slice_in_dim(out_weight, start, columns, axis=1)

    weights = [weight_for(0)] + [shift(weight_for(by), "tensor", by) for by in (1, 3, 2)]

    def at_z(dz, xs=A_ORDER):
        return [lambda x, z, n=n: ((x + n) & (XS - 1)) * ZS + ((z + dz) & (ZS - 1)) for n in xs]

    def at_x(dx, zs=range(ZS)):
        return [lambda x, z, n=n: ((x + dx) & (XS - 1)) * ZS + n for n in zs]

    tie = lax.optimization_barrier
    qb, meta = tie((qb, meta))
    gb = lax.all_to_all(
        jnp.broadcast_to(qb[None], (ZS, HD, WIDE)), "z", split_axis=0, concat_axis=0, tiled=True
    )
    far = [shift(a_r[:, :ROWS], "x", 1), shift(a_l[:, ROWS:], "x", -1)]
    ga = jnp.stack([qa, a_r, a_l, jnp.concatenate(far, axis=1)])
    own_a, own_b = own_attend(qa, qb, own_keys[0], own_values[0])
    pa_up, pa_dn = {}, {}
    up, dn = [ga], [ga]

    def hop(k, blocks=slice(None), blocks_dn=slice(None)):
        up.append(shift(up[k - 1][blocks], "z", 1))
        dn.append(shift(dn[k - 1][blocks_dn], "z", -1))

    def attend_a(k):
        pa_up[k], pa_dn[k] = attend(meta, [up[k], dn[k]], [at_z(-k), at_z(k)], kv)

    hop(1)
    (pa_own,) = attend(meta, [ga], [at_z(0)], kv)
    up[1], dn[1], pa_own, own_a = tie((up[1], dn[1], pa_own, own_a))
    hop(2)
    right, left = shift(gb, "x", 1), shift(gb, "x", -1)
    attend_a(1)
    up[2], dn[2], pa_up[1], pa_dn[1] = tie((up[2], dn[2], pa_up[1], pa_dn[1]))
    hop(3)
    attend_a(2)
    up[3], dn[3], pa_up[2], pa_dn[2] = tie((up[3], dn[3], pa_up[2], pa_dn[2]))
    hop(4, slice(0, 2), slice(2, 4))
    (pb_own,) = attend(meta, [gb], [at_x(0)], kv)
    right, left, pb_own, weights[:2] = tie((right, left, pb_own, weights[:2]))
    right2, left2 = shift(right[:4], "x", 1), shift(left[4:], "x", -1)
    attend_a(3)
    up[4], dn[4], pa_up[3], pa_dn[3] = tie((up[4], dn[4], pa_up[3], pa_dn[3]))
    pa_up[4], pa_dn[4] = attend(
        meta, [up[4], dn[4]], [at_z(4, A_ORDER[:2]), at_z(4, A_ORDER[2:])], kv
    )
    (pb_right,) = attend(meta, [right], [at_x(-1)], kv)
    (pb_left,) = attend(meta, [left], [at_x(1)], kv)
    right2, left2, pb_right, weights[2] = tie((right2, left2, pb_right, weights[2]))
    pb_right2, pb_left2 = attend(
        meta, [right2, left2], [at_x(2, range(4)), at_x(2, range(4, 8))], kv
    )
    pb_right2, pb_left2, weights[3] = tie((pb_right2, pb_left2, weights[3]))

    right, left = shift(pb_right2, "x", -1), shift(pb_left2, "x", 1)
    right, left = join((pb_right, right, 0), (pb_left, left, 4))
    right, left = shift(right, "x", -1), shift(left, "x", 1)
    sum_b = gather(meta, pb_own, right, left, False)

    ups, dns = shift(pa_up[4], "z", -1), shift(pa_dn[4], "z", 1)
    for k, first in ((3, 2), (2, 0), (1, 0)):
        ups, dns = join((pa_up[k], ups, 0), (pa_dn[k], dns, first))
        ups, dns = shift(ups, "z", -1), shift(dns, "z", 1)
    sum_a = gather(meta, pa_own, ups, dns, True)

    came_b = lax.all_to_all(sum_b, "z", split_axis=0, concat_axis=0, tiled=True)
    came_a = lax.all_to_all(sum_a, "x", split_axis=0, concat_axis=0, tiled=True)

    total = residual[0].astype(f32)
    for half, came, own in ((0, came_a, own_a), (1, came_b, own_b)):
        attended = finish(lengths, came, own)
        blocks = [attended] + [shift(attended, "tensor", by) for by in (1, 3, 2)]
        for block, weight in zip(blocks, weights):
            total = total + dot(block, weight[half * 2 * HD : (half + 1) * 2 * HD])
    return total.astype(bf16)[None]


def solution(mesh):
    grid = Mesh(mesh.devices.reshape(XS, ZS, 2, 4), ("x", "z", "core", "tensor"))
    cache = ("x", "z", "core")
    in_specs = (
        P(cache, None, "tensor"),
        P(cache, None, "tensor"),
        P(cache, None, "tensor"),
        P(cache, None, "tensor"),
        P(cache, None, "tensor"),
        P(),
        P(cache, None),
        P(cache),
        P(cache, None, "tensor"),
        P("tensor", None),
    )
    return jax.shard_map(
        on_device,
        mesh=grid,
        in_specs=in_specs,
        out_specs=P(cache, None, "tensor"),
        check_vma=False,
    )
```

```python
import math

import jax
import jax.numpy as jnp
from jax import lax
from jax.experimental import pallas as pl
from jax.experimental.pallas import tpu as pltpu
from jax.sharding import Mesh, PartitionSpec as P

HD = 128
PICKS = 16
PASS_DEV = 16
PLEN = 512
ROWS = 256
WIDE = 2 * ROWS
LANES = 128
DEPTH = 4
A_ORDER = (0, -1, 1, 2)
B_ORDER = (0, -1, 1, -2, 2, -3, 3, 4)
SCALE = 1.0 / math.sqrt(HD)
EXP2_SCALE = SCALE * math.log2(math.e)
EMPTY = -1e30
XS, ZS = 4, 8
REQS_CORE = XS * ZS
TAIL = 32
ONE = HD + 16
bf16, f32 = jnp.bfloat16, jnp.float32
VMEM = pl.BlockSpec(memory_space=pltpu.VMEM)
SMEM = pl.BlockSpec(memory_space=pltpu.SMEM)
ANY = pl.BlockSpec(memory_space=pl.ANY)


def dot(a, b):
    return lax.dot_general(a, b, (((1,), (0,)), ((), ())), preferred_element_type=f32)


def chunk_attend(keys, values_t, queries, visible=None):
    scores = dot(keys, queries)
    if visible is not None:
        scores = jnp.where(visible, scores, EMPTY)
    top = jnp.max(scores, axis=0, keepdims=True)
    e = jnp.exp2((scores - top) * EXP2_SCALE)
    den = jnp.sum(e, axis=0, keepdims=True)
    part = (dot(values_t, e.astype(bf16)) / den).astype(bf16).astype(f32)
    return part, top * SCALE + jnp.log(den)


def weigh(lses):
    top = lses[0]
    for lse in lses[1:]:
        top = jnp.maximum(top, lse)
    weights = [jnp.exp(lse - top) for lse in lses]
    den = weights[0]
    for w in weights[1:]:
        den = den + w
    return [w / den for w in weights], top + jnp.log(den)


def split3(lse):
    hi = lse.astype(bf16).astype(f32)
    mid = (lse - hi).astype(bf16).astype(f32)
    return hi, mid, lse - hi - mid


def message(n):
    return jax.ShapeDtypeStruct((n * HD + TAIL, WIDE), bf16)


def blocks_in(ref):
    return (ref.shape[0] - TAIL) // HD


def block_at(ref, b):
    return ref[b * HD : (b + 1) * HD, :].astype(f32)


def lse_in(ref):
    n = blocks_in(ref) * HD
    tail = ref[n : n + TAIL, :].astype(f32)
    return tail[0:8] + tail[8:16] + tail[16:24]


def put_lse(ref, lse):
    n = blocks_in(ref) * HD
    tail = jnp.concatenate([*split3(lse), jnp.zeros_like(lse)], axis=0)
    ref[n : n + TAIL, :] = tail.astype(bf16)


def attend_kernel(groups, meta, *refs):
    m = len(groups)
    ins = refs[:m]
    kv_own, kv_sib = refs[m : m + 2]
    outs = refs[m + 2 : 2 * m + 2]
    qbuf, kvbuf, acc_s, lse_s, items, qsem, kvsem = refs[2 * m + 2 :]
    offs = [sum(len(g) for g in groups[:i]) for i in range(m)]

    def q_copy(i):
        return pltpu.make_async_copy(
            ins[i], qbuf.at[pl.ds(offs[i], len(groups[i]))], qsem.at[i]
        )

    for i in range(m):
        q_copy(i).start()

    x, z = meta[4 * REQS_CORE], meta[4 * REQS_CORE + 1]
    count = jnp.int32(0)
    for i, group in enumerate(groups):
        for j, request in enumerate(group):
            r = request(x, z)
            s0, s1 = meta[4 * r], meta[4 * r + 1]
            big = (meta[4 * r + 2] > ROWS // 2).astype(jnp.int32)
            kind = (s0 >= 0).astype(jnp.int32) + 2 * (s1 >= 0).astype(jnp.int32)
            items[count] = (
                (offs[i] + j)
                + ((s0 & 15) << 8)
                + ((s1 & 15) << 12)
                + (kind << 16)
                + (big << 18)
                + ((8 * i + j) << 20)
            )
            count = count + (kind > 0).astype(jnp.int32)

            @pl.when(kind == 0)
            def _():
                outs[i][j * HD : (j + 1) * HD, :] = jnp.zeros((HD, WIDE), bf16)

    lse_s[...] = jnp.full(lse_s.shape, EMPTY, f32)

    def kv_copy(ref, slot, buf, pos):
        return pltpu.make_async_copy(ref.at[slot], kvbuf.at[buf, pos], kvsem.at[buf, pos])

    def kv_start(n, buf):
        code = items[n]
        s0, s1, kind = (code >> 8) & 15, (code >> 12) & 15, (code >> 16) & 3

        @pl.when(kind != 2)
        def _():
            kv_copy(kv_own, s0, buf, 0).start()

        @pl.when(kind == 2)
        def _():
            kv_copy(kv_sib, s1, buf, 0).start()

        @pl.when(kind == 3)
        def _():
            kv_copy(kv_sib, s1, buf, 1).start()

    for ahead in range(DEPTH - 1):

        @pl.when(count > ahead)
        def _():
            kv_start(ahead, ahead)

    for i in range(m):
        q_copy(i).wait()

    def step(n, carry):
        buf = n & (DEPTH - 1)

        @pl.when(n + DEPTH - 1 < count)
        def _():
            kv_start(n + DEPTH - 1, (n + DEPTH - 1) & (DEPTH - 1))

        code = items[n]
        b = code & 255
        kind, big, row = (code >> 16) & 3, (code >> 18) & 1, code >> 20

        kv_copy(kv_own, 0, buf, 0).wait()

        @pl.when(kind == 3)
        def _():
            kv_copy(kv_sib, 0, buf, 1).wait()

        def work(picked, starts):
            done = []
            for pos in range(picked):
                keys, values_t = kvbuf[buf, pos, 0], kvbuf[buf, pos, 1].T
                done.append(
                    [chunk_attend(keys, values_t, qbuf[b, :, s : s + LANES]) for s in starts]
                )
            for n_s, s in enumerate(starts):
                if picked == 1:
                    acc, lse = done[0][n_s]
                else:
                    (p0, l0), (p1, l1) = done[0][n_s], done[1][n_s]
                    (w0, w1), lse = weigh([l0, l1])
                    acc = p0 * w0 + p1 * w1
                acc_s[:, s : s + LANES] = acc.astype(bf16)
                lse_s[row, :, s : s + LANES] = lse

        full, short = (0, 128, 256, 384), (0, 256)
        for picked, is_kind in ((1, kind != 3), (2, kind == 3)):

            @pl.when((big == 1) & is_kind)
            def _():
                work(picked, full)

            @pl.when((big == 0) & is_kind)
            def _():
                work(picked, short)
                for s in (128, 384):
                    acc_s[:, s : s + LANES] = jnp.zeros((HD, LANES), bf16)

        for i, group in enumerate(groups):

            @pl.when((b >= offs[i]) & (b < offs[i] + len(group)))
            def _():
                at = pl.multiple_of((b - offs[i]) * HD, HD)
                outs[i][pl.ds(at, HD), :] = acc_s[...]

        return carry

    lax.fori_loop(0, count, step, 0)
    for i in range(m):
        put_lse(outs[i], jnp.concatenate([lse_s[8 * i + j] for j in range(8)], axis=0))


def attend(meta, arrays, groups, kv):
    total = sum(len(g) for g in groups)
    m = len(groups)
    return pl.pallas_call(
        lambda *refs: attend_kernel(groups, *refs),
        out_shape=[message(len(g)) for g in groups],
        in_specs=[SMEM] + [ANY] * (m + 2),
        out_specs=[VMEM] * m,
        scratch_shapes=[
            pltpu.VMEM((total, HD, WIDE), bf16),
            pltpu.VMEM((DEPTH, 2, 2, PLEN, HD), bf16),
            pltpu.VMEM((HD, WIDE), bf16),
            pltpu.VMEM((8 * m, 1, WIDE), f32),
            pltpu.SMEM((total + 1,), jnp.int32),
            pltpu.SemaphoreType.DMA((m,)),
            pltpu.SemaphoreType.DMA((DEPTH, 2)),
        ],
        compiler_params=pltpu.CompilerParams(vmem_limit_bytes=40 * 2**20),
        cost_estimate=pl.CostEstimate(
            flops=total * 4 * PLEN * HD * WIDE,
            bytes_accessed=total * 2**19,
            transcendentals=total * PLEN * WIDE,
        ),
        name="attend",
    )(meta, *arrays, *kv)


def own_kernel(qa, qb, k, v, acc_a, acc_b, lse_a, lse_b):
    key = lax.broadcasted_iota(jnp.int32, (ROWS, LANES), 0)
    row = lax.broadcasted_iota(jnp.int32, (ROWS, LANES), 1)
    keys, values_t = k[...], v[...].T
    for q, acc, lse in ((qa, acc_a, lse_a), (qb, acc_b, lse_b)):
        for s in range(0, WIDE, LANES):
            at = slice(s, s + LANES)
            acc[:, at], lse[:, at] = chunk_attend(
                keys, values_t, q[:, at], key <= row + (s & (ROWS - 1))
            )


def own_attend(qa, qb, k, v):
    acc_a, acc_b, lse_a, lse_b = pl.pallas_call(
        own_kernel,
        out_shape=[jax.ShapeDtypeStruct((HD, WIDE), f32)] * 2
        + [jax.ShapeDtypeStruct((1, WIDE), f32)] * 2,
        in_specs=[VMEM] * 4,
        out_specs=[VMEM] * 4,
        compiler_params=pltpu.CompilerParams(vmem_limit_bytes=32 * 2**20),
        name="own_attend",
    )(qa, qb, k, v)
    return (acc_a, lse_a), (acc_b, lse_b)


def join_kernel(firsts, *refs):
    n = len(firsts)
    for i, first in enumerate(firsts):
        mine, came, out = refs[2 * i], refs[2 * i + 1], refs[2 * n + i]
        count = blocks_in(came)
        lse_m, lse_c = lse_in(mine), lse_in(came)
        if first:
            lse_c = jnp.concatenate(
                [jnp.full((first, WIDE), EMPTY, f32), lse_c[: 8 - first]], axis=0
            )
        (wm, wc), lse = weigh([lse_m, lse_c])
        for b in range(blocks_in(mine)):
            if first <= b < first + count:
                acc = block_at(mine, b) * wm[b : b + 1] + block_at(came, b - first) * wc[b : b + 1]
                out[b * HD : (b + 1) * HD, :] = acc.astype(bf16)
            else:
                out[b * HD : (b + 1) * HD, :] = mine[b * HD : (b + 1) * HD, :]
        put_lse(out, lse)


def join(*triples):
    return pl.pallas_call(
        lambda *refs: join_kernel([t[2] for t in triples], *refs),
        out_shape=[jax.ShapeDtypeStruct(t[0].shape, bf16) for t in triples],
        in_specs=[VMEM] * (2 * len(triples)),
        out_specs=[VMEM] * len(triples),
        compiler_params=pltpu.CompilerParams(vmem_limit_bytes=32 * 2**20),
        name="join",
    )(*[a for t in triples for a in t[:2]])


def gather_kernel(order, meta, a, b, c, out):
    weights, lse = weigh([lse_in(a), lse_in(b), lse_in(c)])
    n_places = len(order)
    place = meta[4 * REQS_CORE] if n_places == XS else meta[4 * REQS_CORE + 1]
    parts = split3(lse)
    for n in range(blocks_in(a)):
        acc = sum(block_at(ref, n) * w[n : n + 1] for ref, w in zip((a, b, c), weights))
        at = (place + order[n]) & (n_places - 1)
        out[at, :HD, :] = acc.astype(bf16)
        tail = [p[n : n + 1] for p in parts] + [jnp.zeros((13, WIDE), f32)]
        out[at, HD:, :] = jnp.concatenate(tail, axis=0).astype(bf16)


def gather(meta, a, b, c, order):
    n = (a.shape[0] - TAIL) // HD
    return pl.pallas_call(
        lambda *refs: gather_kernel(order, *refs),
        out_shape=jax.ShapeDtypeStruct((n, ONE, WIDE), bf16),
        in_specs=[SMEM] + [VMEM] * 3,
        out_specs=VMEM,
        compiler_params=pltpu.CompilerParams(vmem_limit_bytes=32 * 2**20),
        name="gather",
    )(meta, a, b, c)


def finish_kernel(length, came, acc_own, lse_own, out):
    n = came.shape[0]
    lses = [lse_own[...]]
    for i in range(n):
        tail = came[i, HD:, :].astype(f32)
        lses.append(tail[0:1] + tail[1:2] + tail[2:3])
    weights, _ = weigh(lses)
    acc = acc_own[...] * weights[0]
    for i in range(n):
        acc = acc + came[i, :HD, :].astype(f32) * weights[i + 1]
    row = lax.broadcasted_iota(jnp.int32, (HD, WIDE), 1) & (ROWS - 1)
    acc = jnp.where(row < length[0], acc, 0.0)
    for h in range(2):
        out[:, h * HD : (h + 1) * HD] = acc[:, h * ROWS : (h + 1) * ROWS].T.astype(bf16)


def finish(length, came, own):
    return pl.pallas_call(
        finish_kernel,
        out_shape=jax.ShapeDtypeStruct((ROWS, 2 * HD), bf16),
        in_specs=[SMEM, VMEM, VMEM, VMEM],
        out_specs=VMEM,
        compiler_params=pltpu.CompilerParams(vmem_limit_bytes=32 * 2**20),
        name="finish",
    )(length, came, *own)


def shift(value, axis, by):
    n = lax.axis_size(axis)
    return lax.ppermute(value, axis, [(i, (i + by) % n) for i in range(n)])


def on_device(
    queries,
    own_keys,
    own_values,
    passage_keys,
    passage_values,
    passage_slot,
    picks,
    lengths,
    residual,
    out_weight,
):
    x, z, core, t = (lax.axis_index(a) for a in ("x", "z", "core", "tensor"))

    turned = queries[0].reshape(ROWS, 4, HD).transpose(2, 1, 0).reshape(HD, 4 * ROWS)
    qa, qb = turned[:, :WIDE], turned[:, WIDE:]

    storage = jnp.sum(
        jnp.where(
            picks[0][:, None] == jnp.arange(passage_slot.shape[0], dtype=jnp.int32)[None, :],
            passage_slot[None, :],
            0,
        ),
        axis=1,
    )
    told = jnp.concatenate([storage, lengths, jnp.zeros((15,), jnp.int32)])
    a_r, a_l = shift(qa, "x", 1), shift(qa, "x", -1)
    told = lax.all_to_all(
        jnp.broadcast_to(told[None, :], (REQS_CORE, 32)),
        ("x", "z"),
        split_axis=0,
        concat_axis=0,
        tiled=True,
    )
    rows, spans = told[:, :PICKS], told[:, PICKS]
    chip = (x * ZS + z) * 2
    slot0 = jnp.max(jnp.where(rows // PASS_DEV == chip + core, rows % PASS_DEV, -1), axis=1)
    slot1 = jnp.max(jnp.where(rows // PASS_DEV == chip + 1 - core, rows % PASS_DEV, -1), axis=1)
    table = jnp.stack([slot0, slot1, spans, spans], axis=1).reshape(-1)
    place = jnp.stack([x, z, x, z, x, z, x, z]).astype(jnp.int32)
    meta = jnp.concatenate([table, place])
    kv_own = jnp.stack([passage_keys, passage_values], axis=1)
    kv = (kv_own, shift(kv_own, "core", 1))
    a_r, a_l, kv, meta = lax.optimization_barrier((a_r, a_l, kv, meta))


    columns = out_weight.shape[1] // 4

    def weight_for(by):
        start = ((t + by) & 3) * columns
        return lax.dynamic_slice_in_dim(out_weight, start, columns, axis=1)

    weights = [weight_for(0)] + [shift(weight_for(by), "tensor", by) for by in (1, 3, 2)]

    def at_z(dz, xs=A_ORDER):
        return [lambda x, z, n=n: ((x + n) & (XS - 1)) * ZS + ((z + dz) & (ZS - 1)) for n in xs]

    def at_x(dx, zs=B_ORDER):
        return [lambda x, z, n=n: ((x + dx) & (XS - 1)) * ZS + ((z + n) & (ZS - 1)) for n in zs]

    tie = lax.optimization_barrier
    a_far = [shift(a_r[:, :ROWS], "x", 1), shift(a_l[:, ROWS:], "x", -1)]
    b_up, b_dn = [qb], [qb]
    for k in range(3):
        b_up.append(shift(b_up[k], "z", 1))
        b_dn.append(shift(b_dn[k], "z", -1))
        if k == 0:
            b_up[1], b_dn[1], a_far = tie((b_up[1], b_dn[1], a_far))
    far = [shift(b_up[3][:, :ROWS], "z", 1), shift(b_dn[3][:, ROWS:], "z", -1)]
    gb = jnp.stack(
        [qb, b_up[1], b_dn[1], b_up[2], b_dn[2], b_up[3], b_dn[3], jnp.concatenate(far, axis=1)]
    )
    ga = jnp.stack([qa, a_r, a_l, jnp.concatenate(a_far, axis=1)])
    own_a, own_b = own_attend(qa, qb, own_keys[0], own_values[0])
    pa_up, pa_dn = {}, {}
    up, dn = [ga], [ga]

    def hop(k, blocks=slice(None), blocks_dn=slice(None)):
        up.append(shift(up[k - 1][blocks], "z", 1))
        dn.append(shift(dn[k - 1][blocks_dn], "z", -1))

    def attend_a(k):
        pa_up[k], pa_dn[k] = attend(meta, [up[k], dn[k]], [at_z(-k), at_z(k)], kv)

    hop(1)
    right, left = shift(gb, "x", 1), shift(gb, "x", -1)
    (pa_own,) = attend(meta, [ga], [at_z(0)], kv)
    up[1], dn[1], pa_own, weights[1:3] = tie((up[1], dn[1], pa_own, weights[1:3]))
    hop(2)
    (pb_own,) = attend(meta, [gb], [at_x(0)], kv)
    up[2], dn[2], pb_own, own_a = tie((up[2], dn[2], pb_own, own_a))
    hop(3)
    attend_a(1)
    right, left, pa_up[1], pa_dn[1] = tie((right, left, pa_up[1], pa_dn[1]))
    right2, left2 = shift(right[:4], "x", 1), shift(left[4:], "x", -1)
    up[3], dn[3], weights[3] = tie((up[3], dn[3], weights[3]))
    hop(4, slice(0, 2), slice(2, 4))
    attend_a(2)
    (pb_right,) = attend(meta, [right], [at_x(-1)], kv)
    (pb_left,) = attend(meta, [left], [at_x(1)], kv)
    right2, left2, pa_up[2], pa_dn[2], pb_right = tie(
        (right2, left2, pa_up[2], pa_dn[2], pb_right)
    )
    pb_right2, pb_left2 = attend(
        meta, [right2, left2], [at_x(2, B_ORDER[:4]), at_x(2, B_ORDER[4:])], kv
    )
    up[4], dn[4], pb_right2, pb_left2 = tie((up[4], dn[4], pb_right2, pb_left2))
    pa_up[4], pa_dn[4] = attend(
        meta, [up[4], dn[4]], [at_z(4, A_ORDER[:2]), at_z(4, A_ORDER[2:])], kv
    )
    attend_a(3)

    right, left = shift(pb_right2, "x", -1), shift(pb_left2, "x", 1)
    right, left = join((pb_right, right, 0), (pb_left, left, 4))
    right, left = shift(right, "x", -1), shift(left, "x", 1)
    sum_b = gather(meta, pb_own, right, left, B_ORDER)

    ups, dns = shift(pa_up[4], "z", -1), shift(pa_dn[4], "z", 1)
    for k, first in ((3, 2), (2, 0), (1, 0)):
        ups, dns = join((pa_up[k], ups, 0), (pa_dn[k], dns, first))
        ups, dns = shift(ups, "z", -1), shift(dns, "z", 1)
    sum_a = gather(meta, pa_own, ups, dns, A_ORDER)

    came_b = lax.all_to_all(sum_b, "z", split_axis=0, concat_axis=0, tiled=True)
    came_a = lax.all_to_all(sum_a, "x", split_axis=0, concat_axis=0, tiled=True)

    total = residual[0].astype(f32)
    for half, came, own in ((0, came_a, own_a), (1, came_b, own_b)):
        attended = finish(lengths, came, own)
        blocks = [attended] + [shift(attended, "tensor", by) for by in (1, 3, 2)]
        for block, weight in zip(blocks, weights):
            total = total + dot(block, weight[half * 2 * HD : (half + 1) * 2 * HD])
    return total.astype(bf16)[None]


def solution(mesh):
    grid = Mesh(mesh.devices.reshape(XS, ZS, 2, 4), ("x", "z", "core", "tensor"))
    cache = ("x", "z", "core")
    in_specs = (
        P(cache, None, "tensor"),
        P(cache, None, "tensor"),
        P(cache, None, "tensor"),
        P(cache, None, "tensor"),
        P(cache, None, "tensor"),
        P(),
        P(cache, None),
        P(cache),
        P(cache, None, "tensor"),
        P("tensor", None),
    )
    return jax.shard_map(
        on_device,
        mesh=grid,
        in_specs=in_specs,
        out_specs=P(cache, None, "tensor"),
        check_vma=False,
    )
```

```python
import math

import jax
import jax.numpy as jnp
from jax import lax
from jax.experimental import pallas as pl
from jax.experimental.pallas import tpu as pltpu
from jax.sharding import Mesh, PartitionSpec as P

HD = 128
PICKS = 16
PASS_DEV = 16
PLEN = 512
ROWS = 256
WIDE = 2 * ROWS
LANES = 128
DEPTH = 4
A_ORDER = (0, -1, 1, 2)
B_ORDER = (0, -1, 1, -2, 2, -3, 3, 4)
SCALE = 1.0 / math.sqrt(HD)
EXP2_SCALE = SCALE * math.log2(math.e)
EMPTY = -1e30
XS, ZS = 4, 8
REQS_CORE = XS * ZS
TAIL = 32
ONE = HD + 16
bf16, f32 = jnp.bfloat16, jnp.float32
VMEM = pl.BlockSpec(memory_space=pltpu.VMEM)
SMEM = pl.BlockSpec(memory_space=pltpu.SMEM)
ANY = pl.BlockSpec(memory_space=pl.ANY)


def dot(a, b):
    return lax.dot_general(a, b, (((1,), (0,)), ((), ())), preferred_element_type=f32)


def chunk_attend(keys, values_t, queries, visible=None):
    n = keys.shape[0]
    span = min(n, 256)
    tops, dens, outs = [], [], []
    for at in range(0, n, span):
        scores = dot(keys[at : at + span], queries)
        if visible is not None:
            scores = jnp.where(visible, scores, EMPTY)
        top = jnp.max(scores, axis=0, keepdims=True)
        e = jnp.exp2((scores - top) * EXP2_SCALE)
        tops.append(top)
        dens.append(jnp.sum(e, axis=0, keepdims=True))
        outs.append(dot(values_t[:, at : at + span], e.astype(bf16)))
    top, den, out = tops[0], dens[0], outs[0]
    if n > span:
        top = jnp.maximum(tops[0], tops[1])
        w0, w1 = (jnp.exp2((t - top) * EXP2_SCALE) for t in tops)
        den = w0 * dens[0] + w1 * dens[1]
        out = w0 * outs[0] + w1 * outs[1]
    part = (out / den).astype(bf16).astype(f32)
    return part, top * SCALE + jnp.log(den)


def weigh(lses):
    top = lses[0]
    for lse in lses[1:]:
        top = jnp.maximum(top, lse)
    weights = [jnp.exp(lse - top) for lse in lses]
    den = weights[0]
    for w in weights[1:]:
        den = den + w
    return [w / den for w in weights], top + jnp.log(den)


def split3(lse):
    hi = lse.astype(bf16).astype(f32)
    mid = (lse - hi).astype(bf16).astype(f32)
    return hi, mid, lse - hi - mid


def message(n):
    return jax.ShapeDtypeStruct((n * HD + TAIL, WIDE), bf16)


def blocks_in(ref):
    return (ref.shape[0] - TAIL) // HD


def block_at(ref, b):
    return ref[b * HD : (b + 1) * HD, :].astype(f32)


def lse_in(ref):
    n = blocks_in(ref) * HD
    tail = ref[n : n + TAIL, :].astype(f32)
    return tail[0:8] + tail[8:16] + tail[16:24]


def put_lse(ref, lse):
    n = blocks_in(ref) * HD
    tail = jnp.concatenate([*split3(lse), jnp.zeros_like(lse)], axis=0)
    ref[n : n + TAIL, :] = tail.astype(bf16)


def attend_kernel(groups, meta, *refs):
    m = len(groups)
    ins = refs[:m]
    kv_own, kv_sib = refs[m : m + 2]
    outs = refs[m + 2 : 2 * m + 2]
    qbuf, kvbuf, acc_s, lse_s, items, qsem, kvsem = refs[2 * m + 2 :]
    offs = [sum(len(g) for g in groups[:i]) for i in range(m)]

    def q_copy(i):
        return pltpu.make_async_copy(
            ins[i], qbuf.at[pl.ds(offs[i], len(groups[i]))], qsem.at[i]
        )

    for i in range(m):
        q_copy(i).start()

    x, z = meta[4 * REQS_CORE], meta[4 * REQS_CORE + 1]
    count = jnp.int32(0)
    for i, group in enumerate(groups):
        for j, request in enumerate(group):
            r = request(x, z)
            s0, s1 = meta[4 * r], meta[4 * r + 1]
            big = (meta[4 * r + 2] > ROWS // 2).astype(jnp.int32)
            kind = (s0 >= 0).astype(jnp.int32) + 2 * (s1 >= 0).astype(jnp.int32)
            items[count] = (
                (offs[i] + j)
                + ((s0 & 15) << 8)
                + ((s1 & 15) << 12)
                + (kind << 16)
                + (big << 18)
                + ((8 * i + j) << 20)
            )
            count = count + (kind > 0).astype(jnp.int32)

            @pl.when(kind == 0)
            def _():
                outs[i][j * HD : (j + 1) * HD, :] = jnp.zeros((HD, WIDE), bf16)

    lse_s[...] = jnp.full(lse_s.shape, EMPTY, f32)

    def kv_copy(ref, slot, buf, pos):
        return pltpu.make_async_copy(ref.at[slot], kvbuf.at[buf, pos], kvsem.at[buf, pos])

    def kv_start(n, buf):
        code = items[n]
        s0, s1, kind = (code >> 8) & 15, (code >> 12) & 15, (code >> 16) & 3

        @pl.when(kind != 2)
        def _():
            kv_copy(kv_own, s0, buf, 0).start()

        @pl.when(kind == 2)
        def _():
            kv_copy(kv_sib, s1, buf, 0).start()

        @pl.when(kind == 3)
        def _():
            kv_copy(kv_sib, s1, buf, 1).start()

    for ahead in range(DEPTH - 1):

        @pl.when(count > ahead)
        def _():
            kv_start(ahead, ahead)

    for i in range(m):
        q_copy(i).wait()

    def step(n, carry):
        buf = n & (DEPTH - 1)

        @pl.when(n + DEPTH - 1 < count)
        def _():
            kv_start(n + DEPTH - 1, (n + DEPTH - 1) & (DEPTH - 1))

        code = items[n]
        b = code & 255
        kind, big, row = (code >> 16) & 3, (code >> 18) & 1, code >> 20

        kv_copy(kv_own, 0, buf, 0).wait()

        @pl.when(kind == 3)
        def _():
            kv_copy(kv_sib, 0, buf, 1).wait()

        def work(picked, starts):
            done = []
            for pos in range(picked):
                keys, values_t = kvbuf[buf, pos, 0], kvbuf[buf, pos, 1].T
                done.append(
                    [chunk_attend(keys, values_t, qbuf[b, :, s : s + LANES]) for s in starts]
                )
            for n_s, s in enumerate(starts):
                if picked == 1:
                    acc, lse = done[0][n_s]
                else:
                    (p0, l0), (p1, l1) = done[0][n_s], done[1][n_s]
                    (w0, w1), lse = weigh([l0, l1])
                    acc = p0 * w0 + p1 * w1
                acc_s[:, s : s + LANES] = acc.astype(bf16)
                lse_s[row, :, s : s + LANES] = lse

        full, short = (0, 128, 256, 384), (0, 256)
        for picked, is_kind in ((1, kind != 3), (2, kind == 3)):

            @pl.when((big == 1) & is_kind)
            def _():
                work(picked, full)

            @pl.when((big == 0) & is_kind)
            def _():
                work(picked, short)
                for s in (128, 384):
                    acc_s[:, s : s + LANES] = jnp.zeros((HD, LANES), bf16)

        for i, group in enumerate(groups):

            @pl.when((b >= offs[i]) & (b < offs[i] + len(group)))
            def _():
                at = pl.multiple_of((b - offs[i]) * HD, HD)
                outs[i][pl.ds(at, HD), :] = acc_s[...]

        return carry

    lax.fori_loop(0, count, step, 0)
    for i in range(m):
        put_lse(outs[i], jnp.concatenate([lse_s[8 * i + j] for j in range(8)], axis=0))


def attend(meta, arrays, groups, kv):
    total = sum(len(g) for g in groups)
    m = len(groups)
    return pl.pallas_call(
        lambda *refs: attend_kernel(groups, *refs),
        out_shape=[message(len(g)) for g in groups],
        in_specs=[SMEM] + [ANY] * (m + 2),
        out_specs=[VMEM] * m,
        scratch_shapes=[
            pltpu.VMEM((total, HD, WIDE), bf16),
            pltpu.VMEM((DEPTH, 2, 2, PLEN, HD), bf16),
            pltpu.VMEM((HD, WIDE), bf16),
            pltpu.VMEM((8 * m, 1, WIDE), f32),
            pltpu.SMEM((total + 1,), jnp.int32),
            pltpu.SemaphoreType.DMA((m,)),
            pltpu.SemaphoreType.DMA((DEPTH, 2)),
        ],
        compiler_params=pltpu.CompilerParams(vmem_limit_bytes=40 * 2**20),
        cost_estimate=pl.CostEstimate(
            flops=total * 8 * PLEN * HD * WIDE,
            bytes_accessed=total * 2**20,
            transcendentals=total * PLEN * WIDE * 2,
        ),
        name="attend",
    )(meta, *arrays, *kv)


def own_kernel(qa, qb, k, v, acc_a, acc_b, lse_a, lse_b):
    key = lax.broadcasted_iota(jnp.int32, (ROWS, LANES), 0)
    row = lax.broadcasted_iota(jnp.int32, (ROWS, LANES), 1)
    keys, values_t = k[...], v[...].T
    for q, acc, lse in ((qa, acc_a, lse_a), (qb, acc_b, lse_b)):
        for s in range(0, WIDE, LANES):
            at = slice(s, s + LANES)
            acc[:, at], lse[:, at] = chunk_attend(
                keys, values_t, q[:, at], key <= row + (s & (ROWS - 1))
            )


def own_attend(qa, qb, k, v):
    acc_a, acc_b, lse_a, lse_b = pl.pallas_call(
        own_kernel,
        out_shape=[jax.ShapeDtypeStruct((HD, WIDE), f32)] * 2
        + [jax.ShapeDtypeStruct((1, WIDE), f32)] * 2,
        in_specs=[VMEM] * 4,
        out_specs=[VMEM] * 4,
        compiler_params=pltpu.CompilerParams(vmem_limit_bytes=32 * 2**20),
        name="own_attend",
    )(qa, qb, k, v)
    return (acc_a, lse_a), (acc_b, lse_b)


def join_kernel(firsts, *refs):
    n = len(firsts)
    for i, first in enumerate(firsts):
        mine, came, out = refs[2 * i], refs[2 * i + 1], refs[2 * n + i]
        count = blocks_in(came)
        lse_m, lse_c = lse_in(mine), lse_in(came)
        if first:
            lse_c = jnp.concatenate(
                [jnp.full((first, WIDE), EMPTY, f32), lse_c[: 8 - first]], axis=0
            )
        (wm, wc), lse = weigh([lse_m, lse_c])
        for b in range(blocks_in(mine)):
            if first <= b < first + count:
                acc = block_at(mine, b) * wm[b : b + 1] + block_at(came, b - first) * wc[b : b + 1]
                out[b * HD : (b + 1) * HD, :] = acc.astype(bf16)
            else:
                out[b * HD : (b + 1) * HD, :] = mine[b * HD : (b + 1) * HD, :]
        put_lse(out, lse)


def join(*triples):
    return pl.pallas_call(
        lambda *refs: join_kernel([t[2] for t in triples], *refs),
        out_shape=[jax.ShapeDtypeStruct(t[0].shape, bf16) for t in triples],
        in_specs=[VMEM] * (2 * len(triples)),
        out_specs=[VMEM] * len(triples),
        compiler_params=pltpu.CompilerParams(vmem_limit_bytes=32 * 2**20),
        name="join",
    )(*[a for t in triples for a in t[:2]])


def gather_kernel(order, meta, a, b, c, out):
    weights, lse = weigh([lse_in(a), lse_in(b), lse_in(c)])
    n_places = len(order)
    place = meta[4 * REQS_CORE] if n_places == XS else meta[4 * REQS_CORE + 1]
    parts = split3(lse)
    for n in range(blocks_in(a)):
        acc = sum(block_at(ref, n) * w[n : n + 1] for ref, w in zip((a, b, c), weights))
        at = (place + order[n]) & (n_places - 1)
        out[at, :HD, :] = acc.astype(bf16)
        tail = [p[n : n + 1] for p in parts] + [jnp.zeros((13, WIDE), f32)]
        out[at, HD:, :] = jnp.concatenate(tail, axis=0).astype(bf16)


def gather(meta, a, b, c, order):
    n = (a.shape[0] - TAIL) // HD
    return pl.pallas_call(
        lambda *refs: gather_kernel(order, *refs),
        out_shape=jax.ShapeDtypeStruct((n, ONE, WIDE), bf16),
        in_specs=[SMEM] + [VMEM] * 3,
        out_specs=VMEM,
        compiler_params=pltpu.CompilerParams(vmem_limit_bytes=32 * 2**20),
        name="gather",
    )(meta, a, b, c)


def finish_kernel(length, came, acc_own, lse_own, out):
    n = came.shape[0]
    lses = [lse_own[...]]
    for i in range(n):
        tail = came[i, HD:, :].astype(f32)
        lses.append(tail[0:1] + tail[1:2] + tail[2:3])
    weights, _ = weigh(lses)
    acc = acc_own[...] * weights[0]
    for i in range(n):
        acc = acc + came[i, :HD, :].astype(f32) * weights[i + 1]
    row = lax.broadcasted_iota(jnp.int32, (HD, WIDE), 1) & (ROWS - 1)
    acc = jnp.where(row < length[0], acc, 0.0)
    for h in range(2):
        out[:, h * HD : (h + 1) * HD] = acc[:, h * ROWS : (h + 1) * ROWS].T.astype(bf16)


def finish(length, came, own):
    return pl.pallas_call(
        finish_kernel,
        out_shape=jax.ShapeDtypeStruct((ROWS, 2 * HD), bf16),
        in_specs=[SMEM, VMEM, VMEM, VMEM],
        out_specs=VMEM,
        compiler_params=pltpu.CompilerParams(vmem_limit_bytes=32 * 2**20),
        name="finish",
    )(length, came, *own)


def shift(value, axis, by):
    n = lax.axis_size(axis)
    return lax.ppermute(value, axis, [(i, (i + by) % n) for i in range(n)])


def on_device(
    queries,
    own_keys,
    own_values,
    passage_keys,
    passage_values,
    passage_slot,
    picks,
    lengths,
    residual,
    out_weight,
):
    x, z, core, t = (lax.axis_index(a) for a in ("x", "z", "core", "tensor"))

    turned = queries[0].reshape(ROWS, 4, HD).transpose(2, 1, 0).reshape(HD, 4 * ROWS)
    qa, qb = turned[:, :WIDE], turned[:, WIDE:]

    storage = jnp.sum(
        jnp.where(
            picks[0][:, None] == jnp.arange(passage_slot.shape[0], dtype=jnp.int32)[None, :],
            passage_slot[None, :],
            0,
        ),
        axis=1,
    )
    told = jnp.concatenate([storage, lengths, jnp.zeros((15,), jnp.int32)])
    a_r, a_l = shift(qa, "x", 1), shift(qa, "x", -1)
    told = lax.all_to_all(
        jnp.broadcast_to(told[None, :], (REQS_CORE, 32)),
        ("x", "z"),
        split_axis=0,
        concat_axis=0,
        tiled=True,
    )
    rows, spans = told[:, :PICKS], told[:, PICKS]
    chip = (x * ZS + z) * 2
    slot0 = jnp.max(jnp.where(rows // PASS_DEV == chip + core, rows % PASS_DEV, -1), axis=1)
    slot1 = jnp.max(jnp.where(rows // PASS_DEV == chip + 1 - core, rows % PASS_DEV, -1), axis=1)
    table = jnp.stack([slot0, slot1, spans, spans], axis=1).reshape(-1)
    place = jnp.stack([x, z, x, z, x, z, x, z]).astype(jnp.int32)
    meta = jnp.concatenate([table, place])
    kv_own = jnp.stack([passage_keys, passage_values], axis=1)
    kv = (kv_own, shift(kv_own, "core", 1))
    a_r, a_l, kv, meta = lax.optimization_barrier((a_r, a_l, kv, meta))


    columns = out_weight.shape[1] // 4

    def weight_for(by):
        start = ((t + by) & 3) * columns
        return lax.dynamic_slice_in_dim(out_weight, start, columns, axis=1)

    weights = [weight_for(0)] + [shift(weight_for(by), "tensor", by) for by in (1, 3, 2)]

    def at_z(dz, xs=A_ORDER):
        return [lambda x, z, n=n: ((x + n) & (XS - 1)) * ZS + ((z + dz) & (ZS - 1)) for n in xs]

    def at_x(dx, zs=B_ORDER):
        return [lambda x, z, n=n: ((x + dx) & (XS - 1)) * ZS + ((z + n) & (ZS - 1)) for n in zs]

    tie = lax.optimization_barrier
    a_far = [shift(a_r[:, :ROWS], "x", 1), shift(a_l[:, ROWS:], "x", -1)]
    b_up, b_dn = [qb], [qb]
    for k in range(3):
        b_up.append(shift(b_up[k], "z", 1))
        b_dn.append(shift(b_dn[k], "z", -1))
        if k == 0:
            b_up[1], b_dn[1], a_far = tie((b_up[1], b_dn[1], a_far))
    far = [shift(b_up[3][:, :ROWS], "z", 1), shift(b_dn[3][:, ROWS:], "z", -1)]
    gb = jnp.stack(
        [qb, b_up[1], b_dn[1], b_up[2], b_dn[2], b_up[3], b_dn[3], jnp.concatenate(far, axis=1)]
    )
    ga = jnp.stack([qa, a_r, a_l, jnp.concatenate(a_far, axis=1)])
    own_a, own_b = own_attend(qa, qb, own_keys[0], own_values[0])
    pa_up, pa_dn = {}, {}
    up, dn = [ga], [ga]

    def hop(k, blocks=slice(None), blocks_dn=slice(None)):
        up.append(shift(up[k - 1][blocks], "z", 1))
        dn.append(shift(dn[k - 1][blocks_dn], "z", -1))

    def attend_a(k):
        pa_up[k], pa_dn[k] = attend(meta, [up[k], dn[k]], [at_z(-k), at_z(k)], kv)

    hop(1)
    right, left = shift(gb, "x", 1), shift(gb, "x", -1)
    (pa_own,) = attend(meta, [ga], [at_z(0)], kv)
    up[1], dn[1], pa_own, weights[1:3] = tie((up[1], dn[1], pa_own, weights[1:3]))
    hop(2)
    (pb_own,) = attend(meta, [gb], [at_x(0)], kv)
    up[2], dn[2], pb_own, own_a = tie((up[2], dn[2], pb_own, own_a))
    hop(3)
    attend_a(1)
    right, left, pa_up[1], pa_dn[1] = tie((right, left, pa_up[1], pa_dn[1]))
    right2, left2 = shift(right[:4], "x", 1), shift(left[4:], "x", -1)
    up[3], dn[3], weights[3] = tie((up[3], dn[3], weights[3]))
    hop(4, slice(0, 2), slice(2, 4))
    attend_a(2)
    (pb_right,) = attend(meta, [right], [at_x(-1)], kv)
    (pb_left,) = attend(meta, [left], [at_x(1)], kv)
    right2, left2, pa_up[2], pa_dn[2], pb_right = tie(
        (right2, left2, pa_up[2], pa_dn[2], pb_right)
    )
    pb_right2, pb_left2 = attend(
        meta, [right2, left2], [at_x(2, B_ORDER[:4]), at_x(2, B_ORDER[4:])], kv
    )
    up[4], dn[4], pb_right2, pb_left2 = tie((up[4], dn[4], pb_right2, pb_left2))
    pa_up[4], pa_dn[4] = attend(
        meta, [up[4], dn[4]], [at_z(4, A_ORDER[:2]), at_z(4, A_ORDER[2:])], kv
    )
    attend_a(3)

    right, left = shift(pb_right2, "x", -1), shift(pb_left2, "x", 1)
    right, left = join((pb_right, right, 0), (pb_left, left, 4))
    right, left = shift(right, "x", -1), shift(left, "x", 1)
    sum_b = gather(meta, pb_own, right, left, B_ORDER)

    ups, dns = shift(pa_up[4], "z", -1), shift(pa_dn[4], "z", 1)
    for k, first in ((3, 2), (2, 0), (1, 0)):
        ups, dns = join((pa_up[k], ups, 0), (pa_dn[k], dns, first))
        ups, dns = shift(ups, "z", -1), shift(dns, "z", 1)
    sum_a = gather(meta, pa_own, ups, dns, A_ORDER)

    came_b = lax.all_to_all(sum_b, "z", split_axis=0, concat_axis=0, tiled=True)
    came_a = lax.all_to_all(sum_a, "x", split_axis=0, concat_axis=0, tiled=True)

    total = residual[0].astype(f32)
    for half, came, own in ((0, came_a, own_a), (1, came_b, own_b)):
        attended = finish(lengths, came, own)
        blocks = [attended] + [shift(attended, "tensor", by) for by in (1, 3, 2)]
        for block, weight in zip(blocks, weights):
            total = total + dot(block, weight[half * 2 * HD : (half + 1) * 2 * HD])
    return total.astype(bf16)[None]


def solution(mesh):
    grid = Mesh(mesh.devices.reshape(XS, ZS, 2, 4), ("x", "z", "core", "tensor"))
    cache = ("x", "z", "core")
    in_specs = (
        P(cache, None, "tensor"),
        P(cache, None, "tensor"),
        P(cache, None, "tensor"),
        P(cache, None, "tensor"),
        P(cache, None, "tensor"),
        P(),
        P(cache, None),
        P(cache),
        P(cache, None, "tensor"),
        P("tensor", None),
    )
    return jax.shard_map(
        on_device,
        mesh=grid,
        in_specs=in_specs,
        out_specs=P(cache, None, "tensor"),
        check_vma=False,
    )
```

```python
import math

import jax
import jax.numpy as jnp
from jax import lax
from jax.experimental import pallas as pl
from jax.experimental.pallas import tpu as pltpu
from jax.sharding import Mesh, PartitionSpec as P

HD = 128
PICKS = 16
PASS_DEV = 16
PLEN = 512
ROWS = 256
WIDE = 2 * ROWS
LANES = 128
DEPTH = 4
A_ORDER = (0, -1, 1, 2)
B_ORDER = (0, -1, 1, -2, 2, -3, 3, 4)
SCALE = 1.0 / math.sqrt(HD)
EXP2_SCALE = SCALE * math.log2(math.e)
EMPTY = -1e30
XS, ZS = 4, 8
REQS_CORE = XS * ZS
TAIL = 32
ONE = HD + 16
bf16, f32 = jnp.bfloat16, jnp.float32
VMEM = pl.BlockSpec(memory_space=pltpu.VMEM)
SMEM = pl.BlockSpec(memory_space=pltpu.SMEM)
ANY = pl.BlockSpec(memory_space=pl.ANY)


def dot(a, b):
    return lax.dot_general(a, b, (((1,), (0,)), ((), ())), preferred_element_type=f32)


def chunk_attend(keys, values_t, queries, visible=None):
    n = keys.shape[0]
    span = min(n, 256)
    tops, dens, outs = [], [], []
    for at in range(0, n, span):
        scores = dot(keys[at : at + span], queries)
        if visible is not None:
            scores = jnp.where(visible, scores, EMPTY)
        top = jnp.max(scores, axis=0, keepdims=True)
        e = jnp.exp2((scores - top) * EXP2_SCALE)
        tops.append(top)
        dens.append(jnp.sum(e, axis=0, keepdims=True))
        outs.append(dot(values_t[:, at : at + span], e.astype(bf16)))
    if n > span:
        top = jnp.maximum(tops[0], tops[1])
        w0, w1 = (jnp.exp2((t - top) * EXP2_SCALE) for t in tops)
        den = w0 * dens[0] + w1 * dens[1]
        part = outs[0] * (w0 / den) + outs[1] * (w1 / den)
    else:
        top, den = tops[0], dens[0]
        part = outs[0] * (1.0 / den)
    return part.astype(bf16).astype(f32), top * SCALE + jnp.log(den)


def weigh(lses):
    top = lses[0]
    for lse in lses[1:]:
        top = jnp.maximum(top, lse)
    weights = [jnp.exp(lse - top) for lse in lses]
    den = weights[0]
    for w in weights[1:]:
        den = den + w
    return [w / den for w in weights], top + jnp.log(den)


def split3(lse):
    hi = lse.astype(bf16).astype(f32)
    mid = (lse - hi).astype(bf16).astype(f32)
    return hi, mid, lse - hi - mid


def message(n):
    return jax.ShapeDtypeStruct((n * HD + TAIL, WIDE), bf16)


def blocks_in(ref):
    return (ref.shape[0] - TAIL) // HD


def block_at(ref, b):
    return ref[b * HD : (b + 1) * HD, :].astype(f32)


def lse_in(ref):
    n = blocks_in(ref) * HD
    tail = ref[n : n + TAIL, :].astype(f32)
    return tail[0:8] + tail[8:16] + tail[16:24]


def put_lse(ref, lse):
    n = blocks_in(ref) * HD
    tail = jnp.concatenate([*split3(lse), jnp.zeros_like(lse)], axis=0)
    ref[n : n + TAIL, :] = tail.astype(bf16)


def attend_kernel(groups, meta, *refs):
    m = len(groups)
    ins = refs[:m]
    kv_own, kv_sib = refs[m : m + 2]
    outs = refs[m + 2 : 2 * m + 2]
    qbuf, kvbuf, acc_s, lse_s, items, qsem, kvsem = refs[2 * m + 2 :]
    offs = [sum(len(g) for g in groups[:i]) for i in range(m)]

    def q_copy(i):
        return pltpu.make_async_copy(
            ins[i], qbuf.at[pl.ds(offs[i], len(groups[i]))], qsem.at[i]
        )

    for i in range(m):
        q_copy(i).start()

    x, z = meta[4 * REQS_CORE], meta[4 * REQS_CORE + 1]
    count = jnp.int32(0)
    for i, group in enumerate(groups):
        for j, request in enumerate(group):
            r = request(x, z)
            s0, s1 = meta[4 * r], meta[4 * r + 1]
            big = (meta[4 * r + 2] > ROWS // 2).astype(jnp.int32)
            kind = (s0 >= 0).astype(jnp.int32) + 2 * (s1 >= 0).astype(jnp.int32)
            items[count] = (
                (offs[i] + j)
                + ((s0 & 15) << 8)
                + ((s1 & 15) << 12)
                + (kind << 16)
                + (big << 18)
                + ((8 * i + j) << 20)
            )
            count = count + (kind > 0).astype(jnp.int32)

            @pl.when(kind == 0)
            def _():
                outs[i][j * HD : (j + 1) * HD, :] = jnp.zeros((HD, WIDE), bf16)

    lse_s[...] = jnp.full(lse_s.shape, EMPTY, f32)

    def kv_copy(ref, slot, buf, pos):
        return pltpu.make_async_copy(ref.at[slot], kvbuf.at[buf, pos], kvsem.at[buf, pos])

    def kv_start(n, buf):
        code = items[n]
        s0, s1, kind = (code >> 8) & 15, (code >> 12) & 15, (code >> 16) & 3

        @pl.when(kind != 2)
        def _():
            kv_copy(kv_own, s0, buf, 0).start()

        @pl.when(kind == 2)
        def _():
            kv_copy(kv_sib, s1, buf, 0).start()

        @pl.when(kind == 3)
        def _():
            kv_copy(kv_sib, s1, buf, 1).start()

    for ahead in range(DEPTH - 1):

        @pl.when(count > ahead)
        def _():
            kv_start(ahead, ahead)

    for i in range(m):
        q_copy(i).wait()

    def step(n, carry):
        buf = n & (DEPTH - 1)

        @pl.when(n + DEPTH - 1 < count)
        def _():
            kv_start(n + DEPTH - 1, (n + DEPTH - 1) & (DEPTH - 1))

        code = items[n]
        b = code & 255
        kind, big, row = (code >> 16) & 3, (code >> 18) & 1, code >> 20

        kv_copy(kv_own, 0, buf, 0).wait()

        @pl.when(kind == 3)
        def _():
            kv_copy(kv_sib, 0, buf, 1).wait()

        def work(picked, starts):
            done = []
            for pos in range(picked):
                keys, values_t = kvbuf[buf, pos, 0], kvbuf[buf, pos, 1].T
                done.append(
                    [chunk_attend(keys, values_t, qbuf[b, :, s : s + LANES]) for s in starts]
                )
            for n_s, s in enumerate(starts):
                if picked == 1:
                    acc, lse = done[0][n_s]
                else:
                    (p0, l0), (p1, l1) = done[0][n_s], done[1][n_s]
                    (w0, w1), lse = weigh([l0, l1])
                    acc = p0 * w0 + p1 * w1
                acc_s[:, s : s + LANES] = acc.astype(bf16)
                lse_s[row, :, s : s + LANES] = lse

        full, short = (0, 128, 256, 384), (0, 256)
        for picked, is_kind in ((1, kind != 3), (2, kind == 3)):

            @pl.when((big == 1) & is_kind)
            def _():
                work(picked, full)

            @pl.when((big == 0) & is_kind)
            def _():
                work(picked, short)
                for s in (128, 384):
                    acc_s[:, s : s + LANES] = jnp.zeros((HD, LANES), bf16)

        for i, group in enumerate(groups):

            @pl.when((b >= offs[i]) & (b < offs[i] + len(group)))
            def _():
                at = pl.multiple_of((b - offs[i]) * HD, HD)
                outs[i][pl.ds(at, HD), :] = acc_s[...]

        return carry

    lax.fori_loop(0, count, step, 0)
    for i in range(m):
        put_lse(outs[i], jnp.concatenate([lse_s[8 * i + j] for j in range(8)], axis=0))


def attend(meta, arrays, groups, kv):
    total = sum(len(g) for g in groups)
    m = len(groups)
    return pl.pallas_call(
        lambda *refs: attend_kernel(groups, *refs),
        out_shape=[message(len(g)) for g in groups],
        in_specs=[SMEM] + [ANY] * (m + 2),
        out_specs=[VMEM] * m,
        scratch_shapes=[
            pltpu.VMEM((total, HD, WIDE), bf16),
            pltpu.VMEM((DEPTH, 2, 2, PLEN, HD), bf16),
            pltpu.VMEM((HD, WIDE), bf16),
            pltpu.VMEM((8 * m, 1, WIDE), f32),
            pltpu.SMEM((total + 1,), jnp.int32),
            pltpu.SemaphoreType.DMA((m,)),
            pltpu.SemaphoreType.DMA((DEPTH, 2)),
        ],
        compiler_params=pltpu.CompilerParams(vmem_limit_bytes=40 * 2**20),
        cost_estimate=pl.CostEstimate(
            flops=total * 8 * PLEN * HD * WIDE,
            bytes_accessed=total * 2**20,
            transcendentals=total * PLEN * WIDE * 2,
        ),
        name="attend",
    )(meta, *arrays, *kv)


def own_kernel(qa, qb, k, v, acc_a, acc_b, lse_a, lse_b):
    key = lax.broadcasted_iota(jnp.int32, (ROWS, LANES), 0)
    row = lax.broadcasted_iota(jnp.int32, (ROWS, LANES), 1)
    keys, values_t = k[...], v[...].T
    for q, acc, lse in ((qa, acc_a, lse_a), (qb, acc_b, lse_b)):
        for s in range(0, WIDE, LANES):
            at = slice(s, s + LANES)
            acc[:, at], lse[:, at] = chunk_attend(
                keys, values_t, q[:, at], key <= row + (s & (ROWS - 1))
            )


def own_attend(qa, qb, k, v):
    acc_a, acc_b, lse_a, lse_b = pl.pallas_call(
        own_kernel,
        out_shape=[jax.ShapeDtypeStruct((HD, WIDE), f32)] * 2
        + [jax.ShapeDtypeStruct((1, WIDE), f32)] * 2,
        in_specs=[VMEM] * 4,
        out_specs=[VMEM] * 4,
        compiler_params=pltpu.CompilerParams(vmem_limit_bytes=32 * 2**20),
        name="own_attend",
    )(qa, qb, k, v)
    return (acc_a, lse_a), (acc_b, lse_b)


def join_kernel(firsts, *refs):
    n = len(firsts)
    for i, first in enumerate(firsts):
        mine, came, out = refs[2 * i], refs[2 * i + 1], refs[2 * n + i]
        count = blocks_in(came)
        lse_m, lse_c = lse_in(mine), lse_in(came)
        if first:
            lse_c = jnp.concatenate(
                [jnp.full((first, WIDE), EMPTY, f32), lse_c[: 8 - first]], axis=0
            )
        (wm, wc), lse = weigh([lse_m, lse_c])
        for b in range(blocks_in(mine)):
            if first <= b < first + count:
                acc = block_at(mine, b) * wm[b : b + 1] + block_at(came, b - first) * wc[b : b + 1]
                out[b * HD : (b + 1) * HD, :] = acc.astype(bf16)
            else:
                out[b * HD : (b + 1) * HD, :] = mine[b * HD : (b + 1) * HD, :]
        put_lse(out, lse)


def join(*triples):
    return pl.pallas_call(
        lambda *refs: join_kernel([t[2] for t in triples], *refs),
        out_shape=[jax.ShapeDtypeStruct(t[0].shape, bf16) for t in triples],
        in_specs=[VMEM] * (2 * len(triples)),
        out_specs=[VMEM] * len(triples),
        compiler_params=pltpu.CompilerParams(vmem_limit_bytes=32 * 2**20),
        name="join",
    )(*[a for t in triples for a in t[:2]])


def gather_kernel(order, meta, a, b, c, out):
    weights, lse = weigh([lse_in(a), lse_in(b), lse_in(c)])
    n_places = len(order)
    place = meta[4 * REQS_CORE] if n_places == XS else meta[4 * REQS_CORE + 1]
    parts = split3(lse)
    for n in range(blocks_in(a)):
        acc = sum(block_at(ref, n) * w[n : n + 1] for ref, w in zip((a, b, c), weights))
        at = (place + order[n]) & (n_places - 1)
        out[at, :HD, :] = acc.astype(bf16)
        tail = [p[n : n + 1] for p in parts] + [jnp.zeros((13, WIDE), f32)]
        out[at, HD:, :] = jnp.concatenate(tail, axis=0).astype(bf16)


def gather(meta, a, b, c, order):
    n = (a.shape[0] - TAIL) // HD
    return pl.pallas_call(
        lambda *refs: gather_kernel(order, *refs),
        out_shape=jax.ShapeDtypeStruct((n, ONE, WIDE), bf16),
        in_specs=[SMEM] + [VMEM] * 3,
        out_specs=VMEM,
        compiler_params=pltpu.CompilerParams(vmem_limit_bytes=32 * 2**20),
        name="gather",
    )(meta, a, b, c)


def finish_kernel(length, came, acc_own, lse_own, out):
    n = came.shape[0]
    lses = [lse_own[...]]
    for i in range(n):
        tail = came[i, HD:, :].astype(f32)
        lses.append(tail[0:1] + tail[1:2] + tail[2:3])
    weights, _ = weigh(lses)
    acc = acc_own[...] * weights[0]
    for i in range(n):
        acc = acc + came[i, :HD, :].astype(f32) * weights[i + 1]
    row = lax.broadcasted_iota(jnp.int32, (HD, WIDE), 1) & (ROWS - 1)
    acc = jnp.where(row < length[0], acc, 0.0)
    for h in range(2):
        out[:, h * HD : (h + 1) * HD] = acc[:, h * ROWS : (h + 1) * ROWS].T.astype(bf16)


def finish(length, came, own):
    return pl.pallas_call(
        finish_kernel,
        out_shape=jax.ShapeDtypeStruct((ROWS, 2 * HD), bf16),
        in_specs=[SMEM, VMEM, VMEM, VMEM],
        out_specs=VMEM,
        compiler_params=pltpu.CompilerParams(vmem_limit_bytes=32 * 2**20),
        name="finish",
    )(length, came, *own)


def shift(value, axis, by):
    n = lax.axis_size(axis)
    return lax.ppermute(value, axis, [(i, (i + by) % n) for i in range(n)])


def on_device(
    queries,
    own_keys,
    own_values,
    passage_keys,
    passage_values,
    passage_slot,
    picks,
    lengths,
    residual,
    out_weight,
):
    x, z, core, t = (lax.axis_index(a) for a in ("x", "z", "core", "tensor"))

    turned = queries[0].reshape(ROWS, 4, HD).transpose(2, 1, 0).reshape(HD, 4 * ROWS)
    qa, qb = turned[:, :WIDE], turned[:, WIDE:]

    storage = jnp.sum(
        jnp.where(
            picks[0][:, None] == jnp.arange(passage_slot.shape[0], dtype=jnp.int32)[None, :],
            passage_slot[None, :],
            0,
        ),
        axis=1,
    )
    told = jnp.concatenate([storage, lengths, jnp.zeros((15,), jnp.int32)])
    a_r, a_l = shift(qa, "x", 1), shift(qa, "x", -1)
    told = lax.all_to_all(
        jnp.broadcast_to(told[None, :], (REQS_CORE, 32)),
        ("x", "z"),
        split_axis=0,
        concat_axis=0,
        tiled=True,
    )
    rows, spans = told[:, :PICKS], told[:, PICKS]
    chip = (x * ZS + z) * 2
    slot0 = jnp.max(jnp.where(rows // PASS_DEV == chip + core, rows % PASS_DEV, -1), axis=1)
    slot1 = jnp.max(jnp.where(rows // PASS_DEV == chip + 1 - core, rows % PASS_DEV, -1), axis=1)
    table = jnp.stack([slot0, slot1, spans, spans], axis=1).reshape(-1)
    place = jnp.stack([x, z, x, z, x, z, x, z]).astype(jnp.int32)
    meta = jnp.concatenate([table, place])
    kv_own = jnp.stack([passage_keys, passage_values], axis=1)
    kv = (kv_own, shift(kv_own, "core", 1))
    a_r, a_l, kv, meta = lax.optimization_barrier((a_r, a_l, kv, meta))


    columns = out_weight.shape[1] // 4

    def weight_for(by):
        start = ((t + by) & 3) * columns
        return lax.dynamic_slice_in_dim(out_weight, start, columns, axis=1)

    weights = [weight_for(0)] + [shift(weight_for(by), "tensor", by) for by in (1, 3, 2)]

    def at_z(dz, xs=A_ORDER):
        return [lambda x, z, n=n: ((x + n) & (XS - 1)) * ZS + ((z + dz) & (ZS - 1)) for n in xs]

    def at_x(dx, zs=B_ORDER):
        return [lambda x, z, n=n: ((x + dx) & (XS - 1)) * ZS + ((z + n) & (ZS - 1)) for n in zs]

    tie = lax.optimization_barrier
    a_far = [shift(a_r[:, :ROWS], "x", 1), shift(a_l[:, ROWS:], "x", -1)]
    b_up, b_dn = [qb], [qb]
    for k in range(3):
        b_up.append(shift(b_up[k], "z", 1))
        b_dn.append(shift(b_dn[k], "z", -1))
        if k == 0:
            b_up[1], b_dn[1], a_far = tie((b_up[1], b_dn[1], a_far))
    far = [shift(b_up[3][:, :ROWS], "z", 1), shift(b_dn[3][:, ROWS:], "z", -1)]
    gb = jnp.stack(
        [qb, b_up[1], b_dn[1], b_up[2], b_dn[2], b_up[3], b_dn[3], jnp.concatenate(far, axis=1)]
    )
    ga = jnp.stack([qa, a_r, a_l, jnp.concatenate(a_far, axis=1)])
    own_a, own_b = own_attend(qa, qb, own_keys[0], own_values[0])
    pa_up, pa_dn = {}, {}
    up, dn = [ga], [ga]

    def hop(k, blocks=slice(None), blocks_dn=slice(None)):
        up.append(shift(up[k - 1][blocks], "z", 1))
        dn.append(shift(dn[k - 1][blocks_dn], "z", -1))

    def attend_a(k):
        pa_up[k], pa_dn[k] = attend(meta, [up[k], dn[k]], [at_z(-k), at_z(k)], kv)

    hop(1)
    right, left = shift(gb, "x", 1), shift(gb, "x", -1)
    (pa_own,) = attend(meta, [ga], [at_z(0)], kv)
    up[1], dn[1], pa_own, weights[1:3] = tie((up[1], dn[1], pa_own, weights[1:3]))
    hop(2)
    (pb_own,) = attend(meta, [gb], [at_x(0)], kv)
    up[2], dn[2], pb_own, own_a = tie((up[2], dn[2], pb_own, own_a))
    hop(3)
    attend_a(1)
    right, left, pa_up[1], pa_dn[1] = tie((right, left, pa_up[1], pa_dn[1]))
    right2, left2 = shift(right[:4], "x", 1), shift(left[4:], "x", -1)
    up[3], dn[3], weights[3] = tie((up[3], dn[3], weights[3]))
    hop(4, slice(0, 2), slice(2, 4))
    attend_a(2)
    (pb_right,) = attend(meta, [right], [at_x(-1)], kv)
    (pb_left,) = attend(meta, [left], [at_x(1)], kv)
    right2, left2, pa_up[2], pa_dn[2], pb_right = tie(
        (right2, left2, pa_up[2], pa_dn[2], pb_right)
    )
    pb_right2, pb_left2 = attend(
        meta, [right2, left2], [at_x(2, B_ORDER[:4]), at_x(2, B_ORDER[4:])], kv
    )
    up[4], dn[4], pb_right2, pb_left2 = tie((up[4], dn[4], pb_right2, pb_left2))
    pa_up[4], pa_dn[4] = attend(
        meta, [up[4], dn[4]], [at_z(4, A_ORDER[:2]), at_z(4, A_ORDER[2:])], kv
    )
    attend_a(3)

    right, left = shift(pb_right2, "x", -1), shift(pb_left2, "x", 1)
    right, left = join((pb_right, right, 0), (pb_left, left, 4))
    right, left = shift(right, "x", -1), shift(left, "x", 1)
    sum_b = gather(meta, pb_own, right, left, B_ORDER)

    ups, dns = shift(pa_up[4], "z", -1), shift(pa_dn[4], "z", 1)
    for k, first in ((3, 2), (2, 0), (1, 0)):
        ups, dns = join((pa_up[k], ups, 0), (pa_dn[k], dns, first))
        ups, dns = shift(ups, "z", -1), shift(dns, "z", 1)
    sum_a = gather(meta, pa_own, ups, dns, A_ORDER)

    came_b = lax.all_to_all(sum_b, "z", split_axis=0, concat_axis=0, tiled=True)
    came_a = lax.all_to_all(sum_a, "x", split_axis=0, concat_axis=0, tiled=True)

    total = residual[0].astype(f32)
    for half, came, own in ((0, came_a, own_a), (1, came_b, own_b)):
        attended = finish(lengths, came, own)
        blocks = [attended] + [shift(attended, "tensor", by) for by in (1, 3, 2)]
        for block, weight in zip(blocks, weights):
            total = total + dot(block, weight[half * 2 * HD : (half + 1) * 2 * HD])
    return total.astype(bf16)[None]


def solution(mesh):
    grid = Mesh(mesh.devices.reshape(XS, ZS, 2, 4), ("x", "z", "core", "tensor"))
    cache = ("x", "z", "core")
    in_specs = (
        P(cache, None, "tensor"),
        P(cache, None, "tensor"),
        P(cache, None, "tensor"),
        P(cache, None, "tensor"),
        P(cache, None, "tensor"),
        P(),
        P(cache, None),
        P(cache),
        P(cache, None, "tensor"),
        P("tensor", None),
    )
    return jax.shard_map(
        on_device,
        mesh=grid,
        in_specs=in_specs,
        out_specs=P(cache, None, "tensor"),
        check_vma=False,
    )
```
